512 devices in a mesh: dom: 64 (over z, x, core), rep: 8 (over y).
Axes of the slice: x: 4, y: 8, z: 8, core: 2. Of those that a mesh axis runs over, the one named last changes fastest.
Arguments:
- features: bfloat16 [65536, 256], P('dom'), may hold values from -6 to 6
- weight: bfloat16 [256, 256], replicated, may hold values from -0.375 to 0.375
- adjacency: bfloat16 [64, 8, 16, 128, 128], P('dom', 'rep'), may hold values from -0.21875 to 0.21875
- tile_row: int32 [64, 8, 16], P('dom', 'rep'), may hold values from 0 to 7
- tile_column: int32 [64, 8, 16], P('dom', 'rep'), may hold values from 0 to 15
- tile_counts: int32 [64, 8], P('dom', 'rep'), may hold values from 2 to 16, as said below
- send_rows: int32 [64, 8, 64, 16], P('dom', 'rep'), may hold values from 0 to 1023
- send_counts: int32 [64, 8, 64], P('dom', 'rep'), may hold values from 0 to 16, as said below
- cotangent: bfloat16 [65536, 256], P(('dom', 'rep')), may hold values from -24 to 24
Outputs:
- output: bfloat16 [65536, 256], P(('dom', 'rep'))
- feature_grad: bfloat16 [65536, 256], P(('dom', 'rep'))
- weight_grad: float32 [256, 256], P('rep')
The draws below stay inside these ranges and needn't reach their ends.
Inputs may be any that keep to these rules, and one draw needn't show every extreme that they name: Slots t >= tile_counts of a device are padding; one device has all 16 slots live. `send_counts`: A partition sends nothing to itself; every partition at every replica index fills all 16 slots for at least one other partition.
All inputs are finite; a program needn't handle non-finite values.
Results may differ from the reference program's by a relative error of at most 0.0061.
Values may be sent and summed in bfloat16 or wider, within the bound.
A program may use at most 64 MiB of HBM per device.

```python
import jax
import jax.numpy as jnp
from jax import lax

HIDDEN_SIZE = 256
TILE = 128
ROWS = 1024
TILES_DEV = 16
CAP = 16
PARTITIONS = 64
REPLICAS = 8
NODES = 65536
COLTILES = 16


def draw_tile_counts(key, part):
    key = jax.random.fold_in(key, 11)
    count_key, place_key = jax.random.split(key)
    lowest = max(1, TILES_DEV // 8)
    counts = jax.random.randint(count_key, (PARTITIONS, REPLICAS), lowest, TILES_DEV // 2 + 1)
    chosen = jax.random.randint(place_key, (), 0, PARTITIONS * REPLICAS)
    flat_index = jnp.arange(PARTITIONS * REPLICAS).reshape(PARTITIONS, REPLICAS)
    return jnp.where(flat_index == chosen, TILES_DEV, counts).astype(jnp.int32)


def draw_send_counts(key, part):
    key = jax.random.fold_in(key, 23)
    count_key, offset_key = jax.random.split(key)
    counts = jax.random.randint(count_key, (PARTITIONS, REPLICAS, PARTITIONS), 0, CAP + 1)
    offsets = jax.random.randint(offset_key, (PARTITIONS, REPLICAS, 1), 1, PARTITIONS)
    source = jnp.arange(PARTITIONS)[:, None, None]
    target = jnp.arange(PARTITIONS)[None, None, :]
    counts = jnp.where(target == (source + offsets) % PARTITIONS, CAP, counts)
    counts = jnp.where(target == source, 0, counts)
    return counts.astype(jnp.int32)


def touch_ends(drawn, own_key, low, largest):
    dims = drawn.shape
    place = [jax.random.randint(jax.random.fold_in(own_key, axis), (), 0, dims[axis]) for axis in range(len(dims))]
    drawn = drawn.at[tuple(place)].set(low)
    longest = dims.index(max(dims))
    place[longest] = (place[longest] + 1) % dims[longest]
    return drawn.at[tuple(place)].set(largest)


def with_spikes(result, key, source, target, parts, factor):
    def block_of(position):
        return (jnp.arange(result.shape[position]) // (result.shape[position] // parts)).reshape((-1,) + (1,) * (result.ndim - 1 - position))

    first = jax.random.permutation(key, parts)[block_of(target)]
    other_side = (block_of(target) + parts // 2) % parts
    return jnp.where((block_of(source) == first) | (block_of(source) == other_side), factor * result, result)


def shard_levels(own_key, shape, cuts, low, top_value):
    level = 1.0
    for axis_at, parts in cuts:
        heights = jax.random.uniform(jax.random.fold_in(jax.random.fold_in(own_key, 6), axis_at), (parts,), jnp.float32, low / len(cuts), top_value / len(cuts))
        level = level * jnp.repeat(jnp.exp(heights), shape[axis_at] // parts).reshape((-1,) + (1,) * (len(shape) - 1 - axis_at))
    return level


def gaussian(rng, extent, width, reach, cuts=(), held_as=jnp.bfloat16):
    level = shard_levels(rng, extent, cuts, -0.22, 0.18) if cuts else 1.0
    result = jax.random.normal(rng, extent, jnp.float32) * width * level
    return jnp.minimum(jnp.maximum(result, -reach), reach).astype(held_as)


def heavy_noise(rng, extent, scale, most, pieces, heavy, held_as=jnp.bfloat16):
    entries = scale * jax.random.normal(rng, extent, jnp.float32)
    if pieces:
        entries = entries * shard_levels(rng, extent, pieces, -0.22, 0.18)
    return jnp.clip(with_spikes(entries, jax.random.fold_in(rng, 3), *heavy), -most, most).astype(held_as)


def setup_inputs(seed: int = 0) -> dict:
    keys = jax.random.split(jax.random.key(seed), 10)
    features = gaussian(keys[0], (NODES, HIDDEN_SIZE), 1.0, 6.0, ((0, 64),))
    weight = gaussian(keys[1], (HIDDEN_SIZE, HIDDEN_SIZE), HIDDEN_SIZE ** -0.5, 0.375)
    adjacency = gaussian(keys[2], (PARTITIONS, REPLICAS, TILES_DEV, TILE, TILE), (max(1, REPLICAS * TILES_DEV * TILE * TILE // (3 * ROWS))) ** -0.5, 0.21875, ((0, 64), (1, 8)))
    tile_row = touch_ends(jax.random.randint(keys[3], (PARTITIONS, REPLICAS, TILES_DEV), 0, ROWS // TILE), jax.random.fold_in(keys[3], 1), 0, (ROWS // TILE) - 1).astype(jnp.int32)
    tile_column = touch_ends(jax.random.randint(keys[4], (PARTITIONS, REPLICAS, TILES_DEV), 0, COLTILES), jax.random.fold_in(keys[4], 1), 0, COLTILES - 1).astype(jnp.int32)
    tile_counts = draw_tile_counts(jax.random.fold_in(keys[9], 71), 0)
    send_rows = touch_ends(jax.random.randint(keys[6], (PARTITIONS, REPLICAS, PARTITIONS, CAP), 0, ROWS), jax.random.fold_in(keys[6], 1), 0, ROWS - 1).astype(jnp.int32)
    send_counts = draw_send_counts(jax.random.fold_in(keys[9], 71), 0)
    cotangent = heavy_noise(keys[8], (NODES, HIDDEN_SIZE), 1.0, 24.0, ((0, 512),), (0, 1, 256, 6.0))
    return {"features": features, "weight": weight, "adjacency": adjacency, "tile_row": tile_row, "tile_column": tile_column, "tile_counts": tile_counts, "send_rows": send_rows, "send_counts": send_counts, "cotangent": cotangent}


GELU_SCALE = 0.7978845608028654
GELU_CUBIC = 0.044715


def gelu_pair(pre_act):
    inner_arg = GELU_SCALE * (pre_act + GELU_CUBIC * pre_act * pre_act * pre_act)
    tanh_part = jnp.tanh(inner_arg)
    activated = 0.5 * pre_act * (1.0 + tanh_part)
    derivative = 0.5 * (1.0 + tanh_part) + 0.5 * pre_act * (1.0 - tanh_part * tanh_part) * GELU_SCALE * (1.0 + 3.0 * GELU_CUBIC * pre_act * pre_act)
    return activated, derivative


def reference(features, weight, adjacency, tile_row, tile_column, tile_counts, send_rows, send_counts, cotangent):
    feat_blocks = features.reshape(PARTITIONS, ROWS, HIDDEN_SIZE)
    part_index = jnp.arange(PARTITIONS, dtype=jnp.int32)
    slot_index = jnp.arange(CAP, dtype=jnp.int32)
    tile_index = jnp.arange(TILES_DEV, dtype=jnp.int32)
    row_positions = jnp.arange(ROWS // TILE, dtype=jnp.int32)
    column_positions = jnp.arange(COLTILES, dtype=jnp.int32)
    rep_positions = jnp.arange(REPLICAS, dtype=jnp.int32)

    def column_space(dom_index, rep_index):
        row_lists = send_rows[:, rep_index, dom_index]
        slot_live = slot_index[None, :] < send_counts[:, rep_index, dom_index][:, None]
        halo_rows = feat_blocks[part_index[:, None], row_lists]
        halo_rows = jnp.where(slot_live[..., None], halo_rows, jnp.zeros((), features.dtype))
        combined = jnp.concatenate([feat_blocks[dom_index], halo_rows.reshape(PARTITIONS * CAP, HIDDEN_SIZE)], 0)
        return combined.reshape(COLTILES, TILE, HIDDEN_SIZE)

    def forward_device(dom_index, rep_index):
        space_tiles = column_space(dom_index, rep_index)
        picked = space_tiles[tile_column[dom_index, rep_index]].astype(jnp.float32)
        block_vals = adjacency[dom_index, rep_index].astype(jnp.float32)
        products = jnp.einsum("tij,tjf->tif", block_vals, picked, precision=lax.Precision.HIGHEST)
        is_live = tile_index < tile_counts[dom_index, rep_index]
        onehot = ((tile_row[dom_index, rep_index][None, :] == row_positions[:, None]) & is_live[None, :]).astype(jnp.float32)
        summed = jnp.dot(onehot, products.reshape(TILES_DEV, TILE * HIDDEN_SIZE), precision=lax.Precision.HIGHEST)
        return summed.reshape(ROWS, HIDDEN_SIZE)

    def forward_part(dom_index):
        rep_terms = jax.vmap(lambda rep_index: forward_device(dom_index, rep_index))(rep_positions)
        return jnp.sum(rep_terms, axis=0)

    aggregate = lax.map(forward_part, part_index).reshape(NODES, HIDDEN_SIZE).astype(jnp.bfloat16)
    pre_act = jnp.dot(aggregate, weight.T, preferred_element_type=jnp.float32)
    activated, derivative = gelu_pair(pre_act)
    output = activated.astype(jnp.bfloat16)
    pre_grad = (cotangent.astype(jnp.float32) * derivative).astype(jnp.bfloat16)
    weight_grad = jnp.dot(pre_grad.T, aggregate, preferred_element_type=jnp.float32) * (NODES ** -0.5)
    row_grad = jnp.dot(pre_grad, weight, preferred_element_type=jnp.float32).astype(jnp.bfloat16)
    grad_blocks = row_grad.reshape(PARTITIONS, ROWS // TILE, TILE, HIDDEN_SIZE)

    def backward_device(dom_index, rep_index):
        picked = grad_blocks[dom_index][tile_row[dom_index, rep_index]].astype(jnp.float32)
        block_vals = adjacency[dom_index, rep_index].astype(jnp.float32)
        products = jnp.einsum("tij,tif->tjf", block_vals, picked, precision=lax.Precision.HIGHEST)
        is_live = tile_index < tile_counts[dom_index, rep_index]
        onehot = ((tile_column[dom_index, rep_index][None, :] == column_positions[:, None]) & is_live[None, :]).astype(jnp.float32)
        summed = jnp.dot(onehot, products.reshape(TILES_DEV, TILE * HIDDEN_SIZE), precision=lax.Precision.HIGHEST)
        return summed.reshape(COLTILES * TILE, HIDDEN_SIZE)

    def backward_part(carried, dom_index):
        space_grads = jax.vmap(lambda rep_index: backward_device(dom_index, rep_index))(rep_positions)
        carried = carried.at[dom_index].add(jnp.sum(space_grads[:, :ROWS], axis=0))
        halo_grads = space_grads[:, ROWS:].reshape(REPLICAS, PARTITIONS, CAP, HIDDEN_SIZE)
        row_lists = jnp.transpose(send_rows[:, :, dom_index], (1, 0, 2))
        counts = jnp.transpose(send_counts[:, :, dom_index], (1, 0))
        slot_live = slot_index[None, None, :] < counts[:, :, None]
        halo_grads = jnp.where(slot_live[..., None], halo_grads, jnp.zeros((), halo_grads.dtype))
        owners = jnp.broadcast_to(part_index[None, :, None], row_lists.shape)
        carried = carried.at[owners, row_lists].add(halo_grads)
        return carried, None

    feature_sums, unused = lax.scan(backward_part, jnp.zeros((PARTITIONS, ROWS, HIDDEN_SIZE), jnp.float32), part_index)
    feature_grad = feature_sums.reshape(NODES, HIDDEN_SIZE).astype(jnp.bfloat16)
    return output, feature_grad, weight_grad
```

```python
import functools

import jax
import jax.numpy as jnp
from jax import lax
from jax.experimental import pallas as pl
from jax.experimental.pallas import tpu as pltpu
from jax.sharding import PartitionSpec as P

GELU_SCALE = 0.7978845608028654
GELU_CUBIC = 0.044715
MESH = pl.DeviceIdType.MESH
TILE = 128
CAP = 16
F32 = jnp.float32
BF16 = jnp.bfloat16


def gelu_pair(pre_act):
    inner_arg = GELU_SCALE * (pre_act + GELU_CUBIC * pre_act * pre_act * pre_act)
    tanh_part = jnp.tanh(inner_arg)
    activated = 0.5 * pre_act * (1.0 + tanh_part)
    derivative = 0.5 * (1.0 + tanh_part) + 0.5 * pre_act * (
        1.0 - tanh_part * tanh_part
    ) * GELU_SCALE * (1.0 + 3.0 * GELU_CUBIC * pre_act * pre_act)
    return (activated, derivative)


def loop(start, stop, body):
    def step(k, carry):
        body(k)
        return carry

    lax.fori_loop(start, stop, step, 0)


def kernel(
    doms,
    reps,
    scale,
    features,
    weight,
    adjacency,
    slots,
    tile_row,
    tile_column,
    tile_count,
    cotangent,
    output,
    feature_grad,
    weight_grad,
    space,
    outgoing,
    scatter,
    a_cat,
    at_cat,
    row_lanes,
    column_lanes,
    picked,
    agg_send,
    agg_recv,
    row_grads,
    back_send,
    back_recv,
    feature_part,
    feat_send,
    feat_recv,
    w_send,
    w_recv,
    w_sum,
    w_rep,
    w_done,
    send_sems,
    recv_sems,
):
    d = lax.axis_index("dom")
    r = lax.axis_index("rep")
    rows, hidden = features.shape
    tiles = adjacency.shape[0]
    row_tiles = rows // TILE
    blocks = doms * CAP // TILE
    per = TILE // CAP
    first_halo = rows // CAP
    HALO, AGG, GRAD, BACK, FEAT, W_DOM, W_REP, W_END = range(8)

    barrier = pltpu.get_barrier_semaphore()

    def greet_dom(k):
        pl.semaphore_signal(
            barrier, inc=1, device_id={"dom": lax.rem(d + k, doms)}, device_id_type=MESH
        )

    def greet_rep(k):
        pl.semaphore_signal(
            barrier, inc=1, device_id={"rep": lax.rem(r + k, reps)}, device_id_type=MESH
        )

    loop(1, doms, greet_dom)
    loop(1, reps, greet_rep)

    def push(src, dst, phase, target):
        pltpu.make_async_remote_copy(
            src_ref=src,
            dst_ref=dst,
            send_sem=send_sems.at[phase],
            recv_sem=recv_sems.at[phase],
            device_id=target,
            device_id_type=MESH,
        ).start()

    def await_bytes(ref, sems, phase):
        pltpu.make_async_copy(ref, ref, sems.at[phase]).wait()

    def send_block(block, src, dst, phase):
        def send(j):
            q = block * per + j

            @pl.when(q != d)
            def _():
                push(src.at[q], dst, phase, {"dom": q})

        loop(0, per, send)

    lane = lax.broadcasted_iota(jnp.int32, (TILE, TILE), 1)

    def gather(b):
        block = lax.rem(d // per + b, blocks)
        listed = jnp.broadcast_to(slots[pl.ds(block, 1), :], (TILE, TILE)).T
        onehot = jnp.concatenate(
            [jnp.where(listed == lane + i * TILE, 1.0, 0.0).astype(BF16) for i in range(row_tiles)],
            axis=1,
        )
        picked_rows = jnp.dot(onehot, features[...], preferred_element_type=F32).astype(BF16)
        outgoing[pl.ds(block * per, per)] = picked_rows.reshape(per, CAP, hidden)

    gather(0)
    pl.semaphore_wait(barrier, doms + reps - 2)
    send_block(d // per, outgoing, space.at[first_halo + d], HALO)

    def gather_and_send(b):
        gather(b)
        send_block(lax.rem(d // per + b, blocks), outgoing, space.at[first_halo + d], HALO)

    loop(1, blocks, gather_and_send)

    space[pl.ds(0, first_halo)] = features[...].reshape(first_halo, CAP, hidden)
    space[first_halo + d] = jnp.zeros((CAP, hidden), BF16)
    back_recv[d] = jnp.zeros((CAP, hidden), BF16)
    for t in range(tiles):
        lanes = slice(t * TILE, (t + 1) * TILE)
        live = t < tile_count[0]
        row_lanes[:, lanes] = jnp.full((CAP, TILE), jnp.where(live, tile_row[t], -1), jnp.int32)
        column_lanes[:, lanes] = jnp.full(
            (CAP, TILE), jnp.where(live, tile_column[t], -1), jnp.int32
        )
        a_cat[:, :, lanes] = adjacency[t].reshape(per, CAP, TILE)
        at_cat[:, :, lanes] = adjacency[t].T.reshape(per, CAP, TILE)
    row = lax.broadcasted_iota(jnp.int32, (TILE, TILE), 0)

    def make_scatter(i):
        for block in range(blocks):
            listed = jnp.broadcast_to(slots[block : block + 1, :], (TILE, TILE))
            scatter[i, :, block * TILE : (block + 1) * TILE] = jnp.where(
                listed == row + i * TILE, 1.0, 0.0
            ).astype(BF16)

    loop(0, row_tiles, make_scatter)

    def tile_sum(values, lanes, index):
        mask = jnp.where(lanes[...] == index, 1.0, 0.0).astype(BF16)
        masked = (values[...] * mask[None]).reshape(TILE, tiles * TILE)
        return jnp.dot(masked, picked[...], preferred_element_type=F32)

    await_bytes(space.at[pl.ds(first_halo, doms - 1)], recv_sems, HALO)
    for t in range(tiles):
        picked[t * TILE : (t + 1) * TILE, :] = space[pl.ds(tile_column[t] * per, per)].reshape(
            TILE, hidden
        )

    def forward(k):
        i = lax.rem(r + k, reps)
        agg_send[i] = tile_sum(a_cat, row_lanes, i).astype(BF16)
        push(agg_send.at[i], agg_recv.at[r], AGG, {"rep": i})

    loop(1, reps, forward)
    total = tile_sum(a_cat, row_lanes, r)
    await_bytes(agg_recv.at[pl.ds(0, reps - 1)], recv_sems, AGG)
    for k in range(1, reps):
        total = total + agg_recv[lax.rem(r + k, reps)].astype(F32)
    aggregate = total.astype(BF16)

    pre_act = lax.dot_general(
        aggregate, weight[...], (((1,), (1,)), ((), ())), preferred_element_type=F32
    )
    activated, derivative = gelu_pair(pre_act)
    pre_grad = (cotangent[...].astype(F32) * derivative).astype(BF16)
    row_grads[r] = jnp.dot(pre_grad, weight[...], preferred_element_type=F32).astype(BF16)

    def share_rows(k):
        push(row_grads.at[r], row_grads.at[r], GRAD, {"rep": lax.rem(r + k, reps)})

    loop(1, reps, share_rows)
    output[...] = activated.astype(BF16)

    w_part = lax.dot_general(
        pre_grad, aggregate, (((0,), (0,)), ((), ())), preferred_element_type=F32
    )
    chunk = w_send.shape[1]
    half = doms // 2
    for h in range(2):
        w_send[h * half : (h + 1) * half] = w_part[:, h * TILE : (h + 1) * TILE].reshape(
            half, chunk, TILE
        )

    def share_weight(k):
        q = lax.rem(d + k, doms)
        push(w_send.at[q], w_recv.at[d], W_DOM, {"dom": q})

    loop(1, doms, share_weight)
    w_recv[d] = w_send[d]

    await_bytes(row_grads.at[pl.ds(0, reps - 1)], recv_sems, GRAD)
    for t in range(tiles):
        picked[t * TILE : (t + 1) * TILE, :] = row_grads[tile_row[t]]

    def backward_halo(b):
        block = lax.rem(d // per + b, blocks)
        grads = tile_sum(at_cat, column_lanes, block + row_tiles).astype(BF16)
        back_send[pl.ds(block * per, per)] = grads.reshape(per, CAP, hidden)
        send_block(block, back_send, back_recv.at[d], BACK)

    loop(0, blocks, backward_halo)

    spread = half // reps
    holder = lax.rem(d, half) // spread
    place = (d // half) * spread + lax.rem(d, spread)
    await_bytes(w_recv.at[pl.ds(0, doms - 1)], recv_sems, W_DOM)
    w_sum[...] = jnp.sum(w_recv[...], axis=0)

    @pl.when(r != holder)
    def _():
        push(w_sum, w_rep.at[r], W_REP, {"rep": holder})

    def backward_local(i):
        feature_part[i] = tile_sum(at_cat, column_lanes, i)

    loop(0, row_tiles, backward_local)

    @pl.when(r == holder)
    def _():
        await_bytes(w_rep.at[pl.ds(0, reps - 1)], recv_sems, W_REP)
        whole = w_sum[...]
        for k in range(1, reps):
            whole = whole + w_rep[lax.rem(r + k, reps)]
        w_done[place] = whole * scale

        def share_done(k):
            push(w_done.at[place], w_done.at[place], W_END, {"dom": lax.rem(d + k, doms)})

        loop(1, doms, share_done)

    await_bytes(back_recv.at[pl.ds(0, doms - 1)], recv_sems, BACK)

    def feature_rows(i):
        returned = back_recv[...].reshape(doms * CAP, hidden)
        return feature_part[i] + jnp.dot(scatter[i], returned, preferred_element_type=F32)

    def feature(k):
        i = lax.rem(r + k, reps)
        feat_send[i] = feature_rows(i).astype(BF16)
        push(feat_send.at[i], feat_recv.at[r], FEAT, {"rep": i})

    loop(1, reps, feature)
    own = feature_rows(r)

    @pl.when(r == holder)
    def _():
        await_bytes(w_done.at[pl.ds(0, 2 * spread - 1)], recv_sems, W_END)

    @pl.when(r != holder)
    def _():
        await_bytes(w_done, recv_sems, W_END)

    for h in range(2):
        weight_grad[:, h * TILE : (h + 1) * TILE] = w_done[h * spread : (h + 1) * spread].reshape(
            spread * chunk, TILE
        )

    await_bytes(feat_recv.at[pl.ds(0, reps - 1)], recv_sems, FEAT)
    for k in range(1, reps):
        own = own + feat_recv[lax.rem(r + k, reps)].astype(F32)
    feature_grad[...] = own.astype(BF16)

    await_bytes(outgoing.at[pl.ds(0, doms - 1)], send_sems, HALO)
    await_bytes(agg_send.at[pl.ds(0, reps - 1)], send_sems, AGG)
    await_bytes(row_grads.at[pl.ds(0, reps - 1)], send_sems, GRAD)
    await_bytes(back_send.at[pl.ds(0, doms - 1)], send_sems, BACK)
    await_bytes(feat_send.at[pl.ds(0, reps - 1)], send_sems, FEAT)
    await_bytes(w_send.at[pl.ds(0, doms - 1)], send_sems, W_DOM)

    @pl.when(r != holder)
    def _():
        await_bytes(w_sum, send_sems, W_REP)

    @pl.when(r == holder)
    def _():
        await_bytes(w_send.at[pl.ds(0, doms - 1)], send_sems, W_END)


def solution(mesh):
    doms, reps = mesh.shape["dom"], mesh.shape["rep"]

    def local(
        features,
        weight,
        adjacency,
        tile_row,
        tile_column,
        tile_counts,
        send_rows,
        send_counts,
        cotangent,
    ):
        rows, hidden = features.shape
        tiles = adjacency.shape[2]
        row_tiles = rows // TILE
        blocks = doms * CAP // TILE
        chunk = 2 * hidden // doms
        slot_live = jnp.arange(CAP)[None, :] < send_counts[0, 0][:, None]
        slots = jnp.where(slot_live, send_rows[0, 0], -1).reshape(blocks, TILE)
        vmem = pl.BlockSpec(memory_space=pltpu.VMEM)
        smem = pl.BlockSpec(memory_space=pltpu.SMEM)
        return pl.pallas_call(
            functools.partial(kernel, doms, reps, float(rows * doms) ** (-0.5)),
            out_shape=(
                jax.ShapeDtypeStruct((rows // reps, hidden), BF16),
                jax.ShapeDtypeStruct((rows // reps, hidden), BF16),
                jax.ShapeDtypeStruct((hidden // reps, hidden), F32),
            ),
            in_specs=[vmem] * 4 + [smem] * 3 + [vmem],
            out_specs=(vmem, vmem, vmem),
            scratch_shapes=[
                pltpu.VMEM((rows // CAP + doms, CAP, hidden), BF16),
                pltpu.VMEM((doms, CAP, hidden), BF16),
                pltpu.VMEM((row_tiles, TILE, doms * CAP), BF16),
                pltpu.VMEM((TILE // CAP, CAP, tiles * TILE), BF16),
                pltpu.VMEM((TILE // CAP, CAP, tiles * TILE), BF16),
                pltpu.VMEM((CAP, tiles * TILE), jnp.int32),
                pltpu.VMEM((CAP, tiles * TILE), jnp.int32),
                pltpu.VMEM((tiles * TILE, hidden), BF16),
                pltpu.VMEM((reps, TILE, hidden), BF16),
                pltpu.VMEM((reps, TILE, hidden), BF16),
                pltpu.VMEM((reps, TILE, hidden), BF16),
                pltpu.VMEM((doms, CAP, hidden), BF16),
                pltpu.VMEM((doms, CAP, hidden), BF16),
                pltpu.VMEM((row_tiles, TILE, hidden), F32),
                pltpu.VMEM((reps, TILE, hidden), BF16),
                pltpu.VMEM((reps, TILE, hidden), BF16),
                pltpu.VMEM((doms, chunk, TILE), F32),
                pltpu.VMEM((doms, chunk, TILE), F32),
                pltpu.VMEM((chunk, TILE), F32),
                pltpu.VMEM((reps, chunk, TILE), F32),
                pltpu.VMEM((doms // reps, chunk, TILE), F32),
                pltpu.SemaphoreType.DMA((8,)),
                pltpu.SemaphoreType.DMA((8,)),
            ],
            compiler_params=pltpu.CompilerParams(
                collective_id=0, has_side_effects=True, vmem_limit_bytes=40 * 2**20
            ),
        )(
            features,
            weight,
            adjacency[0, 0],
            slots,
            tile_row[0, 0],
            tile_column[0, 0],
            tile_counts[0],
            cotangent,
        )

    in_specs = (
        P("dom", None),
        P(),
        P("dom", "rep", None, None, None),
        P("dom", "rep", None),
        P("dom", "rep", None),
        P("dom", "rep"),
        P("dom", "rep", None, None),
        P("dom", "rep", None),
        P(("dom", "rep"), None),
    )
    out_specs = (P(("dom", "rep"), None), P(("dom", "rep"), None), P("rep", None))
    return jax.shard_map(local, mesh=mesh, in_specs=in_specs, out_specs=out_specs, check_vma=False)
```

```python
import functools

import jax
import jax.numpy as jnp
from jax import lax
from jax.experimental import pallas as pl
from jax.experimental.pallas import tpu as pltpu
from jax.sharding import PartitionSpec as P

GELU_SCALE = 0.7978845608028654
GELU_CUBIC = 0.044715
MESH = pl.DeviceIdType.MESH
TILE = 128
CAP = 16
F32 = jnp.float32
BF16 = jnp.bfloat16


def gelu_pair(pre_act):
    inner_arg = GELU_SCALE * (pre_act + GELU_CUBIC * pre_act * pre_act * pre_act)
    tanh_part = jnp.tanh(inner_arg)
    activated = 0.5 * pre_act * (1.0 + tanh_part)
    derivative = 0.5 * (1.0 + tanh_part) + 0.5 * pre_act * (
        1.0 - tanh_part * tanh_part
    ) * GELU_SCALE * (1.0 + 3.0 * GELU_CUBIC * pre_act * pre_act)
    return (activated, derivative)


def loop(start, stop, body):
    def step(k, carry):
        body(k)
        return carry

    lax.fori_loop(start, stop, step, 0)


def kernel(
    doms,
    reps,
    scale,
    features_in,
    weight_in,
    adjacency_in,
    lists_in,
    list_counts_in,
    tile_row_in,
    tile_column_in,
    tile_count_in,
    cotangent_in,
    output,
    feature_grad,
    weight_grad,
    features,
    weight,
    adjacency,
    lists,
    list_counts,
    tile_row,
    tile_column,
    tile_count,
    cotangent,
    listed,
    space_low,
    space_high,
    outgoing,
    scatter,
    a_cat,
    at_cat,
    by_row,
    by_column,
    row_lanes,
    column_lanes,
    picked,
    agg_send,
    agg_recv,
    row_grads_low,
    row_grads_high,
    back_send,
    back_recv,
    feature_part,
    feat_send,
    feat_recv,
    w_send,
    w_recv,
    w_sum,
    w_rep,
    w_done,
    copy_sems,
    send_sems,
    recv_sems,
):
    d = lax.axis_index("dom")
    r = lax.axis_index("rep")
    rows, hidden = features.shape
    tiles = adjacency.shape[0]
    row_tiles = rows // TILE
    blocks = doms * CAP // TILE
    per = TILE // CAP
    first_halo = rows // CAP
    halves = hidden // TILE
    space = (space_low, space_high)
    row_grads = (row_grads_low, row_grads_high)
    HALO, AGG, GRAD, BACK, FEAT = (halves * k for k in range(5))
    W_DOM, W_REP, W_END = (halves * 5 + k for k in range(3))

    barrier = pltpu.get_barrier_semaphore()

    def greet_dom(k):
        pl.semaphore_signal(
            barrier, inc=1, device_id={"dom": lax.rem(d + k, doms)}, device_id_type=MESH
        )

    def greet_rep(k):
        pl.semaphore_signal(
            barrier, inc=1, device_id={"rep": lax.rem(r + k, reps)}, device_id_type=MESH
        )

    loop(1, doms, greet_dom)
    loop(1, reps, greet_rep)

    loads = [
        pltpu.make_async_copy(src, dst, copy_sems.at[k])
        for k, (src, dst) in enumerate(
            (
                (lists_in.at[0, 0], lists),
                (list_counts_in.at[0], list_counts),
                (features_in, features),
                (adjacency_in.at[0, 0], adjacency),
                (tile_row_in, tile_row),
                (tile_column_in, tile_column),
                (tile_count_in, tile_count),
                (weight_in, weight),
                (cotangent_in, cotangent),
            )
        )
    ]
    for load in loads:
        load.start()

    def push(src, dst, phase, target):
        pltpu.make_async_remote_copy(
            src_ref=src,
            dst_ref=dst,
            send_sem=send_sems.at[phase],
            recv_sem=recv_sems.at[phase],
            device_id=target,
            device_id_type=MESH,
        ).start()

    def await_bytes(ref, sems, phase):
        pltpu.make_async_copy(ref, ref, sems.at[phase]).wait()

    def send_block(block, src, dst, phase):
        def send(j):
            q = block * per + j

            @pl.when(q != d)
            def _():
                push(src.at[q], dst, phase, {"dom": q})

        loop(0, per, send)

    def far_block(b):
        step = (2 * lax.rem(b, 2) - 1) * ((b + 1) // 2)
        return lax.rem(d // per + blocks // 2 + step + 2 * blocks, blocks)

    far_reps = sorted(range(1, reps), key=lambda k: -min(k, reps - k))

    lane = lax.broadcasted_iota(jnp.int32, (TILE, TILE), 1)
    row = lax.broadcasted_iota(jnp.int32, (TILE, TILE), 0)
    for load in loads[:3]:
        load.wait()
    slot = lax.broadcasted_iota(jnp.int32, (CAP, doms), 0)
    live_lists = jnp.where(slot < list_counts[...], lists[...], -1)
    for p in range(doms):
        listed[p // per, p % per * CAP : (p % per + 1) * CAP, :] = jnp.broadcast_to(
            live_lists[:, p : p + 1], (CAP, TILE)
        )

    def gather(block):
        rows_of = listed[block]
        onehot = jnp.concatenate(
            [jnp.where(rows_of == lane + i * TILE, 1.0, 0.0).astype(BF16) for i in range(row_tiles)],
            axis=1,
        )
        found = jnp.dot(onehot, features[...], preferred_element_type=F32).astype(BF16)
        for h in range(halves):
            outgoing[h, pl.ds(block * per, per)] = found[:, h * TILE : (h + 1) * TILE].reshape(
                per, CAP, TILE
            )

    def send_halo(block, h):
        send_block(block, outgoing.at[h], space[h].at[first_halo + d], HALO + h)

    gather(far_block(0))
    pl.semaphore_wait(barrier, doms + reps - 2)
    send_halo(far_block(0), 0)

    def gather_and_send(b):
        block = far_block(b)
        gather(block)
        send_halo(block, 0)

    loop(1, blocks, gather_and_send)
    for h in range(1, halves):
        loop(0, blocks, lambda b: send_halo(far_block(b), h))

    for load in loads[3:]:
        load.wait()
    for t in range(tiles):
        lanes = slice(t * TILE, (t + 1) * TILE)
        live = t < tile_count[0, 0]
        row_lanes[:, lanes] = jnp.full(
            (CAP, TILE), jnp.where(live, tile_row[0, 0, t], -1), jnp.int32
        )
        column_lanes[:, lanes] = jnp.full(
            (CAP, TILE), jnp.where(live, tile_column[0, 0, t], -1), jnp.int32
        )
        a_cat[:, :, lanes] = adjacency[t].reshape(per, CAP, TILE)
        at_cat[:, :, lanes] = adjacency[t].T.reshape(per, CAP, TILE)

    def mask_tiles(dst, values, lanes):
        def one(i):
            mask = jnp.where(lanes[...] == i, 1.0, 0.0).astype(BF16)
            dst[i] = (values[...] * mask[None]).reshape(TILE, tiles * TILE)

        loop(0, dst.shape[0], one)

    mask_tiles(by_row, a_cat, row_lanes)
    for h in range(halves):
        space[h][pl.ds(0, first_halo)] = features[:, h * TILE : (h + 1) * TILE].reshape(
            first_halo, CAP, TILE
        )
        space[h][first_halo + d] = jnp.zeros((CAP, TILE), BF16)
        back_recv[h, d] = jnp.zeros((CAP, TILE), BF16)
    mask_tiles(by_column, at_cat, column_lanes)

    def make_scatter(block):
        rows_of = listed[block].T
        for i in range(row_tiles):
            scatter[i, block] = jnp.where(rows_of == row + i * TILE, 1.0, 0.0).astype(BF16)

    loop(0, blocks, make_scatter)

    def tile_sum(values, h):
        return jnp.dot(values, picked[h], preferred_element_type=F32)

    own = []
    for h in range(halves):
        await_bytes(space[h].at[pl.ds(first_halo, doms - 1)], recv_sems, HALO + h)
        for t in range(tiles):
            picked[h, t * TILE : (t + 1) * TILE, :] = space[h][
                pl.ds(tile_column[0, 0, t] * per, per)
            ].reshape(TILE, TILE)
        for k in far_reps:
            i = lax.rem(r + k, reps)
            agg_send[h, i] = tile_sum(by_row[i], h).astype(BF16)
            push(agg_send.at[h, i], agg_recv.at[h, r], AGG + h, {"rep": i})
        own.append(tile_sum(by_row[r], h))

    def rep_sum(total, received, phase, h):
        await_bytes(received.at[h, pl.ds(0, reps - 1)], recv_sems, phase + h)
        for k in range(1, reps):
            total = total + received[h, lax.rem(r + k, reps)].astype(F32)
        return total

    aggregate = jnp.concatenate(
        [rep_sum(own[h], agg_recv, AGG, h).astype(BF16) for h in range(halves)], axis=1
    )

    pre_act = lax.dot_general(
        aggregate, weight[...], (((1,), (1,)), ((), ())), preferred_element_type=F32
    )
    activated, derivative = gelu_pair(pre_act)
    pre_grad = (cotangent[...].astype(F32) * derivative).astype(BF16)
    for h in range(halves):
        row_grads[h][r] = jnp.dot(
            pre_grad, weight[:, h * TILE : (h + 1) * TILE], preferred_element_type=F32
        ).astype(BF16)
        for k in far_reps:
            push(
                row_grads[h].at[r], row_grads[h].at[r], GRAD + h, {"rep": lax.rem(r + k, reps)}
            )
    output[...] = activated.astype(BF16)

    w_part = lax.dot_general(
        pre_grad, aggregate, (((0,), (0,)), ((), ())), preferred_element_type=F32
    )
    chunk = w_send.shape[1]
    half = doms // 2
    for h in range(2):
        w_send[h * half : (h + 1) * half] = w_part[:, h * TILE : (h + 1) * TILE].reshape(
            half, chunk, TILE
        )
    loop(0, blocks, lambda b: send_block(far_block(b), w_send, w_recv.at[d], W_DOM))
    w_recv[d] = w_send[d]

    for h in range(halves):
        await_bytes(row_grads[h].at[pl.ds(0, reps - 1)], recv_sems, GRAD + h)
        for t in range(tiles):
            picked[h, t * TILE : (t + 1) * TILE, :] = row_grads[h][tile_row[0, 0, t]]

        def backward_halo(b):
            block = far_block(b)
            grads = tile_sum(by_column[block + row_tiles], h).astype(BF16)
            back_send[h, pl.ds(block * per, per)] = grads.reshape(per, CAP, TILE)
            send_block(block, back_send.at[h], back_recv.at[h, d], BACK + h)

        loop(0, blocks, backward_halo)

    spread = half // reps
    holder = lax.rem(d, half) // spread
    place = (d // half) * spread + lax.rem(d, spread)
    await_bytes(w_recv.at[pl.ds(0, doms - 1)], recv_sems, W_DOM)
    w_sum[...] = jnp.sum(w_recv[...], axis=0)

    @pl.when(r != holder)
    def _():
        push(w_sum, w_rep.at[r], W_REP, {"rep": holder})

    for h in range(halves):

        def backward_local(i):
            feature_part[h, i] = tile_sum(by_column[i], h)

        loop(0, row_tiles, backward_local)

    @pl.when(r == holder)
    def _():
        await_bytes(w_rep.at[pl.ds(0, reps - 1)], recv_sems, W_REP)
        whole = w_sum[...]
        for k in range(1, reps):
            whole = whole + w_rep[lax.rem(r + k, reps)]
        w_done[place] = whole * scale

        def share_done(k):
            push(w_done.at[place], w_done.at[place], W_END, {"dom": lax.rem(d + k, doms)})

        loop(1, doms, share_done)

    own = []
    for h in range(halves):
        await_bytes(back_recv.at[h, pl.ds(0, doms - 1)], recv_sems, BACK + h)

        def feature_rows(i):
            total = feature_part[h, i]
            for block in range(blocks):
                returned = back_recv[h, block * per : (block + 1) * per].reshape(TILE, TILE)
                total = total + jnp.dot(scatter[i, block], returned, preferred_element_type=F32)
            return total

        for k in far_reps:
            i = lax.rem(r + k, reps)
            feat_send[h, i] = feature_rows(i).astype(BF16)
            push(feat_send.at[h, i], feat_recv.at[h, r], FEAT + h, {"rep": i})
        own.append(feature_rows(r))

    @pl.when(r == holder)
    def _():
        await_bytes(w_done.at[pl.ds(0, 2 * spread - 1)], recv_sems, W_END)

    @pl.when(r != holder)
    def _():
        await_bytes(w_done, recv_sems, W_END)

    for h in range(2):
        weight_grad[:, h * TILE : (h + 1) * TILE] = w_done[h * spread : (h + 1) * spread].reshape(
            spread * chunk, TILE
        )
    for h in range(halves):
        feature_grad[:, h * TILE : (h + 1) * TILE] = rep_sum(own[h], feat_recv, FEAT, h).astype(
            BF16
        )

    for h in range(halves):
        await_bytes(outgoing.at[h, pl.ds(0, doms - 1)], send_sems, HALO + h)
        await_bytes(agg_send.at[h, pl.ds(0, reps - 1)], send_sems, AGG + h)
        await_bytes(row_grads[h].at[pl.ds(0, reps - 1)], send_sems, GRAD + h)
        await_bytes(back_send.at[h, pl.ds(0, doms - 1)], send_sems, BACK + h)
        await_bytes(feat_send.at[h, pl.ds(0, reps - 1)], send_sems, FEAT + h)
    await_bytes(w_send.at[pl.ds(0, doms - 1)], send_sems, W_DOM)

    @pl.when(r != holder)
    def _():
        await_bytes(w_sum, send_sems, W_REP)

    @pl.when(r == holder)
    def _():
        await_bytes(w_send.at[pl.ds(0, doms - 1)], send_sems, W_END)


def solution(mesh):
    doms, reps = mesh.shape["dom"], mesh.shape["rep"]

    def local(
        features,
        weight,
        adjacency,
        tile_row,
        tile_column,
        tile_counts,
        send_rows,
        send_counts,
        cotangent,
    ):
        rows, hidden = features.shape
        tiles = adjacency.shape[2]
        row_tiles = rows // TILE
        blocks = doms * CAP // TILE
        halves = hidden // TILE
        chunk = 2 * hidden // doms
        vmem = pl.BlockSpec(memory_space=pltpu.VMEM)
        hbm = pl.BlockSpec(memory_space=pltpu.HBM)
        i32 = jnp.int32
        phases = halves * 5 + 3
        scratch = (
            ((rows, hidden), BF16),
            ((hidden, hidden), BF16),
            ((tiles, TILE, TILE), BF16),
            ((CAP, doms), i32),
            ((1, doms), i32),
            (pltpu.SMEM, (1, 1, tiles), i32),
            (pltpu.SMEM, (1, 1, tiles), i32),
            (pltpu.SMEM, (1, 1), i32),
            ((rows // reps, hidden), BF16),
            ((blocks, TILE, TILE), i32),
            ((rows // CAP + doms, CAP, TILE), BF16),
            ((rows // CAP + doms, CAP, TILE), BF16),
            ((halves, doms, CAP, TILE), BF16),
            ((row_tiles, blocks, TILE, TILE), BF16),
            ((TILE // CAP, CAP, tiles * TILE), BF16),
            ((TILE // CAP, CAP, tiles * TILE), BF16),
            ((row_tiles, TILE, tiles * TILE), BF16),
            ((row_tiles + blocks, TILE, tiles * TILE), BF16),
            ((CAP, tiles * TILE), i32),
            ((CAP, tiles * TILE), i32),
            ((halves, tiles * TILE, TILE), BF16),
            ((halves, reps, TILE, TILE), BF16),
            ((halves, reps, TILE, TILE), BF16),
            ((reps, TILE, TILE), BF16),
            ((reps, TILE, TILE), BF16),
            ((halves, doms, CAP, TILE), BF16),
            ((halves, doms, CAP, TILE), BF16),
            ((halves, row_tiles, TILE, TILE), F32),
            ((halves, reps, TILE, TILE), BF16),
            ((halves, reps, TILE, TILE), BF16),
            ((doms, chunk, TILE), F32),
            ((doms, chunk, TILE), F32),
            ((chunk, TILE), F32),
            ((reps, chunk, TILE), F32),
            ((doms // reps, chunk, TILE), F32),
        )
        return pl.pallas_call(
            functools.partial(kernel, doms, reps, float(rows * doms) ** (-0.5)),
            out_shape=(
                jax.ShapeDtypeStruct((rows // reps, hidden), BF16),
                jax.ShapeDtypeStruct((rows // reps, hidden), BF16),
                jax.ShapeDtypeStruct((hidden // reps, hidden), F32),
            ),
            in_specs=[hbm] * 9,
            out_specs=(vmem, vmem, vmem),
            scratch_shapes=[
                item[0](*item[1:]) if len(item) == 3 else pltpu.VMEM(*item) for item in scratch
            ]
            + [
                pltpu.SemaphoreType.DMA((9,)),
                pltpu.SemaphoreType.DMA((phases,)),
                pltpu.SemaphoreType.DMA((phases,)),
            ],
            compiler_params=pltpu.CompilerParams(
                collective_id=0, has_side_effects=True, vmem_limit_bytes=60 * 2**20
            ),
        )(
            features,
            weight,
            adjacency,
            jnp.swapaxes(send_rows, 2, 3),
            send_counts,
            tile_row,
            tile_column,
            tile_counts,
            cotangent,
        )

    in_specs = (
        P("dom", None),
        P(),
        P("dom", "rep", None, None, None),
        P("dom", "rep", None),
        P("dom", "rep", None),
        P("dom", "rep"),
        P("dom", "rep", None, None),
        P("dom", "rep", None),
        P(("dom", "rep"), None),
    )
    out_specs = (P(("dom", "rep"), None), P(("dom", "rep"), None), P("rep", None))
    return jax.shard_map(local, mesh=mesh, in_specs=in_specs, out_specs=out_specs, check_vma=False)
```

```python
import functools

import jax
import jax.numpy as jnp
from jax import lax
from jax.experimental import pallas as pl
from jax.experimental.pallas import tpu as pltpu
from jax.sharding import PartitionSpec as P

GELU_SCALE = 0.7978845608028654
GELU_CUBIC = 0.044715
MESH = pl.DeviceIdType.MESH
TILE = 128
CAP = 16
F32 = jnp.float32
BF16 = jnp.bfloat16


def gelu_pair(pre_act):
    inner_arg = GELU_SCALE * (pre_act + GELU_CUBIC * pre_act * pre_act * pre_act)
    tanh_part = jnp.tanh(inner_arg)
    activated = 0.5 * pre_act * (1.0 + tanh_part)
    derivative = 0.5 * (1.0 + tanh_part) + 0.5 * pre_act * (
        1.0 - tanh_part * tanh_part
    ) * GELU_SCALE * (1.0 + 3.0 * GELU_CUBIC * pre_act * pre_act)
    return (activated, derivative)


def loop(start, stop, body):
    def step(k, carry):
        body(k)
        return carry

    lax.fori_loop(start, stop, step, 0)


def kernel(
    doms,
    reps,
    scale,
    features_in,
    weight_in,
    adjacency_in,
    lists_in,
    list_counts_in,
    tile_row_in,
    tile_column_in,
    tile_count_in,
    cotangent_in,
    output,
    feature_grad,
    weight_grad,
    features,
    weight,
    adjacency,
    lists,
    list_counts,
    tile_row,
    tile_column,
    tile_count,
    cotangent,
    listed,
    space_low,
    space_high,
    outgoing,
    scatter,
    a_cat,
    at_cat,
    by_row,
    by_column,
    row_lanes,
    column_lanes,
    picked,
    agg_send,
    agg_recv,
    own_sum,
    aggregate,
    pre_grad,
    row_grads_low,
    row_grads_high,
    back_send,
    back_recv,
    feature_part,
    feat_send,
    feat_recv,
    w_send,
    w_recv,
    w_sum,
    w_rep,
    w_done,
    copy_sems,
    send_sems,
    recv_sems,
):
    d = lax.axis_index("dom")
    r = lax.axis_index("rep")
    rows, hidden = features.shape
    tiles = adjacency.shape[0]
    row_tiles = rows // TILE
    blocks = doms * CAP // TILE
    per = TILE // CAP
    first_halo = rows // CAP
    halves = hidden // TILE
    space = (space_low, space_high)
    row_grads = (row_grads_low, row_grads_high)
    HALO, AGG, GRAD, BACK, FEAT = (halves * k for k in range(5))
    W_DOM, W_REP, W_END, AGG_LAST = (halves * 5 + k for k in range(4))

    barrier = pltpu.get_barrier_semaphore()

    def greet_dom(k):
        pl.semaphore_signal(
            barrier, inc=1, device_id={"dom": lax.rem(d + k, doms)}, device_id_type=MESH
        )

    def greet_rep(k):
        pl.semaphore_signal(
            barrier, inc=1, device_id={"rep": lax.rem(r + k, reps)}, device_id_type=MESH
        )

    loads = [
        pltpu.make_async_copy(src, dst, copy_sems.at[k])
        for k, (src, dst) in enumerate(
            (
                (lists_in.at[0, 0], lists),
                (list_counts_in.at[0], list_counts),
                (features_in, features),
                (adjacency_in.at[0, 0], adjacency),
                (tile_row_in, tile_row),
                (tile_column_in, tile_column),
                (tile_count_in, tile_count),
                (weight_in, weight),
                (cotangent_in, cotangent),
            )
        )
    ]
    for load in loads[:3]:
        load.start()
    loop(doms // 2, doms, greet_dom)
    loop(1, doms // 2, greet_dom)
    loop(1, reps, greet_rep)
    for load in loads[3:]:
        load.start()

    def push(src, dst, phase, target):
        pltpu.make_async_remote_copy(
            src_ref=src,
            dst_ref=dst,
            send_sem=send_sems.at[phase],
            recv_sem=recv_sems.at[phase],
            device_id=target,
            device_id_type=MESH,
        ).start()

    def await_bytes(ref, sems, phase):
        pltpu.make_async_copy(ref, ref, sems.at[phase]).wait()

    def send_block(block, src, dst, phase):
        def send(j):
            q = block * per + j

            @pl.when(q != d)
            def _():
                push(src.at[q], dst, phase, {"dom": q})

        loop(0, per, send)

    def far_block(b):
        step = (2 * lax.rem(b, 2) - 1) * ((b + 1) // 2)
        return lax.rem(d // per + blocks // 2 + step + 2 * blocks, blocks)

    far_reps = sorted(range(1, reps), key=lambda k: -min(k, reps - k))

    def share_rows(h, k, c):
        size = TILE // 2
        mine = row_grads[h].at[r, c * size : (c + 1) * size]
        push(mine, mine, GRAD + h, {"rep": lax.rem(r + k, reps)})

    lane = lax.broadcasted_iota(jnp.int32, (TILE, TILE), 1)
    row = lax.broadcasted_iota(jnp.int32, (TILE, TILE), 0)
    for load in loads[:3]:
        load.wait()
    slot = lax.broadcasted_iota(jnp.int32, (CAP, doms), 0)
    live_lists = jnp.where(slot < list_counts[...], lists[...], -1)
    for p in range(doms):
        listed[p // per, p % per * CAP : (p % per + 1) * CAP, :] = jnp.broadcast_to(
            live_lists[:, p : p + 1], (CAP, TILE)
        )

    def gather(block):
        rows_of = listed[block]
        onehot = jnp.concatenate(
            [jnp.where(rows_of == lane + i * TILE, 1.0, 0.0).astype(BF16) for i in range(row_tiles)],
            axis=1,
        )
        found = jnp.dot(onehot, features[...], preferred_element_type=F32).astype(BF16)
        for h in range(halves):
            outgoing[h, pl.ds(block * per, per)] = found[:, h * TILE : (h + 1) * TILE].reshape(
                per, CAP, TILE
            )

    def send_halo(block, h):
        send_block(block, outgoing.at[h], space[h].at[first_halo + d], HALO + h)

    loop(0, blocks, gather)
    pl.semaphore_wait(barrier, doms + reps - 2)
    for h in range(halves):
        loop(0, blocks, lambda b: send_halo(far_block(b), h))

    for load in loads[3:]:
        load.wait()
    for t in range(tiles):
        lanes = slice(t * TILE, (t + 1) * TILE)
        live = t < tile_count[0, 0]
        row_lanes[:, lanes] = jnp.full(
            (CAP, TILE), jnp.where(live, tile_row[0, 0, t], -1), jnp.int32
        )
        column_lanes[:, lanes] = jnp.full(
            (CAP, TILE), jnp.where(live, tile_column[0, 0, t], -1), jnp.int32
        )
        a_cat[:, :, lanes] = adjacency[t].reshape(per, CAP, TILE)
        at_cat[:, :, lanes] = adjacency[t].T.reshape(per, CAP, TILE)

    def mask_tiles(dst, values, lanes):
        def one(i):
            mask = jnp.where(lanes[...] == i, 1.0, 0.0).astype(BF16)
            dst[i] = (values[...] * mask[None]).reshape(TILE, tiles * TILE)

        loop(0, dst.shape[0], one)

    mask_tiles(by_row, a_cat, row_lanes)
    for h in range(halves):
        space[h][pl.ds(0, first_halo)] = features[:, h * TILE : (h + 1) * TILE].reshape(
            first_halo, CAP, TILE
        )
        space[h][first_halo + d] = jnp.zeros((CAP, TILE), BF16)
        back_recv[h, d] = jnp.zeros((CAP, TILE), BF16)
    mask_tiles(by_column, at_cat, column_lanes)

    def make_scatter(block):
        rows_of = listed[block].T
        for i in range(row_tiles):
            scatter[i, block] = jnp.where(rows_of == row + i * TILE, 1.0, 0.0).astype(BF16)

    loop(0, blocks, make_scatter)

    def tile_sum(values, h):
        return jnp.dot(values, picked[h], preferred_element_type=F32)

    pieces = 2
    piece_rows = TILE // pieces
    piece_at = [slice(c * piece_rows, (c + 1) * piece_rows) for c in range(pieces)]
    last = halves - 1

    def send_piece(h, i, c):
        push(
            agg_send.at[h, i, piece_at[c]],
            agg_recv.at[h, r, piece_at[c]],
            AGG_LAST + c if h == last else AGG + h,
            {"rep": i},
        )

    for h in range(halves):
        await_bytes(space[h].at[pl.ds(first_halo, doms - 1)], recv_sems, HALO + h)
        for t in range(tiles):
            picked[h, t * TILE : (t + 1) * TILE, :] = space[h][
                pl.ds(tile_column[0, 0, t] * per, per)
            ].reshape(TILE, TILE)
        for k in far_reps:
            i = lax.rem(r + k, reps)
            agg_send[h, i] = tile_sum(by_row[i], h).astype(BF16)
            if h == last:
                send_piece(h, i, 0)
            else:
                push(agg_send.at[h, i], agg_recv.at[h, r], AGG + h, {"rep": i})
        if h == last:
            for c in range(1, pieces):
                for k in far_reps:
                    send_piece(h, lax.rem(r + k, reps), c)
        own_sum[h] = tile_sum(by_row[r], h)

    for h in range(last):
        await_bytes(agg_recv.at[h, pl.ds(0, reps - 1)], recv_sems, AGG + h)
        for k in range(1, reps):
            own_sum[h] += agg_recv[h, lax.rem(r + k, reps)].astype(F32)
    for c in range(pieces):
        await_bytes(agg_recv.at[last, pl.ds(0, reps - 1), piece_at[c]], recv_sems, AGG_LAST + c)
        total = own_sum[last, piece_at[c]]
        for k in range(1, reps):
            total = total + agg_recv[last, lax.rem(r + k, reps), piece_at[c]].astype(F32)
        piece = jnp.concatenate(
            [own_sum[h, piece_at[c]].astype(BF16) for h in range(last)] + [total.astype(BF16)],
            axis=1,
        )
        aggregate[piece_at[c]] = piece
        pre_act = lax.dot_general(
            piece, weight[...], (((1,), (1,)), ((), ())), preferred_element_type=F32
        )
        activated, derivative = gelu_pair(pre_act)
        grad = (cotangent[piece_at[c]].astype(F32) * derivative).astype(BF16)
        pre_grad[piece_at[c]] = grad
        output[piece_at[c]] = activated.astype(BF16)
        row_grad = jnp.dot(grad, weight[...], preferred_element_type=F32).astype(BF16)
        for h in range(halves):
            row_grads[h][r, piece_at[c]] = row_grad[:, h * TILE : (h + 1) * TILE]
        for k in far_reps:
            share_rows(0, k, c)
    for h in range(1, halves):
        for c in range(pieces):
            for k in far_reps:
                share_rows(h, k, c)

    w_part = lax.dot_general(
        pre_grad[...], aggregate[...], (((0,), (0,)), ((), ())), preferred_element_type=F32
    )
    chunk = w_send.shape[1]
    half = doms // 2
    for h in range(2):
        w_send[h * half : (h + 1) * half] = w_part[:, h * TILE : (h + 1) * TILE].reshape(
            half, chunk, TILE
        )
    loop(0, blocks, lambda b: send_block(far_block(b), w_send, w_recv.at[d], W_DOM))
    w_recv[d] = w_send[d]

    for h in range(halves):
        await_bytes(row_grads[h].at[pl.ds(0, reps - 1)], recv_sems, GRAD + h)
        for t in range(tiles):
            picked[h, t * TILE : (t + 1) * TILE, :] = row_grads[h][tile_row[0, 0, t]]

        def backward_halo(b):
            block = far_block(b)
            grads = tile_sum(by_column[block + row_tiles], h).astype(BF16)
            back_send[h, pl.ds(block * per, per)] = grads.reshape(per, CAP, TILE)
            send_block(block, back_send.at[h], back_recv.at[h, d], BACK + h)

        loop(0, blocks, backward_halo)

    spread = half // reps
    holder = lax.rem(d, half) // spread
    place = (d // half) * spread + lax.rem(d, spread)
    await_bytes(w_recv.at[pl.ds(0, doms - 1)], recv_sems, W_DOM)
    w_sum[...] = jnp.sum(w_recv[...], axis=0)

    @pl.when(r != holder)
    def _():
        push(w_sum, w_rep.at[r], W_REP, {"rep": holder})

    for h in range(halves):

        def backward_local(i):
            feature_part[h, i] = tile_sum(by_column[i], h)

        loop(0, row_tiles, backward_local)

    @pl.when(r == holder)
    def _():
        await_bytes(w_rep.at[pl.ds(0, reps - 1)], recv_sems, W_REP)
        whole = w_sum[...]
        for k in range(1, reps):
            whole = whole + w_rep[lax.rem(r + k, reps)]
        w_done[place] = whole * scale

        def share_done(k):
            push(w_done.at[place], w_done.at[place], W_END, {"dom": lax.rem(d + k, doms)})

        loop(1, doms, share_done)

    own = []
    for h in range(halves):
        await_bytes(back_recv.at[h, pl.ds(0, doms - 1)], recv_sems, BACK + h)

        def feature_rows(i):
            total = feature_part[h, i]
            for block in range(blocks):
                returned = back_recv[h, block * per : (block + 1) * per].reshape(TILE, TILE)
                total = total + jnp.dot(scatter[i, block], returned, preferred_element_type=F32)
            return total

        for k in far_reps:
            i = lax.rem(r + k, reps)
            feat_send[h, i] = feature_rows(i).astype(BF16)
            push(feat_send.at[h, i], feat_recv.at[h, r], FEAT + h, {"rep": i})
        own.append(feature_rows(r))

    @pl.when(r == holder)
    def _():
        await_bytes(w_done.at[pl.ds(0, 2 * spread - 1)], recv_sems, W_END)

    @pl.when(r != holder)
    def _():
        await_bytes(w_done, recv_sems, W_END)

    for h in range(2):
        weight_grad[:, h * TILE : (h + 1) * TILE] = w_done[h * spread : (h + 1) * spread].reshape(
            spread * chunk, TILE
        )
    for h in range(halves):
        await_bytes(feat_recv.at[h, pl.ds(0, reps - 1)], recv_sems, FEAT + h)
        total = own[h]
        for k in range(1, reps):
            total = total + feat_recv[h, lax.rem(r + k, reps)].astype(F32)
        feature_grad[:, h * TILE : (h + 1) * TILE] = total.astype(BF16)

    for h in range(halves):
        await_bytes(outgoing.at[h, pl.ds(0, doms - 1)], send_sems, HALO + h)
        if h != last:
            await_bytes(agg_send.at[h, pl.ds(0, reps - 1)], send_sems, AGG + h)
        await_bytes(row_grads[h].at[pl.ds(0, reps - 1)], send_sems, GRAD + h)
        await_bytes(back_send.at[h, pl.ds(0, doms - 1)], send_sems, BACK + h)
        await_bytes(feat_send.at[h, pl.ds(0, reps - 1)], send_sems, FEAT + h)
    for c in range(pieces):
        await_bytes(agg_send.at[last, pl.ds(0, reps - 1), piece_at[c]], send_sems, AGG_LAST + c)
    await_bytes(w_send.at[pl.ds(0, doms - 1)], send_sems, W_DOM)

    @pl.when(r != holder)
    def _():
        await_bytes(w_sum, send_sems, W_REP)

    @pl.when(r == holder)
    def _():
        await_bytes(w_send.at[pl.ds(0, doms - 1)], send_sems, W_END)


def solution(mesh):
    doms, reps = mesh.shape["dom"], mesh.shape["rep"]

    def local(
        features,
        weight,
        adjacency,
        tile_row,
        tile_column,
        tile_counts,
        send_rows,
        send_counts,
        cotangent,
    ):
        rows, hidden = features.shape
        tiles = adjacency.shape[2]
        row_tiles = rows // TILE
        blocks = doms * CAP // TILE
        halves = hidden // TILE
        chunk = 2 * hidden // doms
        vmem = pl.BlockSpec(memory_space=pltpu.VMEM)
        hbm = pl.BlockSpec(memory_space=pltpu.HBM)
        i32 = jnp.int32
        phases = halves * 5 + 5
        out_shape = (
            jax.ShapeDtypeStruct((rows // reps, hidden), BF16),
            jax.ShapeDtypeStruct((rows // reps, hidden), BF16),
            jax.ShapeDtypeStruct((hidden // reps, hidden), F32),
        )
        scratch = (
            ((rows, hidden), BF16),
            ((hidden, hidden), BF16),
            ((tiles, TILE, TILE), BF16),
            ((CAP, doms), i32),
            ((1, doms), i32),
            (pltpu.SMEM, (1, 1, tiles), i32),
            (pltpu.SMEM, (1, 1, tiles), i32),
            (pltpu.SMEM, (1, 1), i32),
            ((rows // reps, hidden), BF16),
            ((blocks, TILE, TILE), i32),
            ((rows // CAP + doms, CAP, TILE), BF16),
            ((rows // CAP + doms, CAP, TILE), BF16),
            ((halves, doms, CAP, TILE), BF16),
            ((row_tiles, blocks, TILE, TILE), BF16),
            ((TILE // CAP, CAP, tiles * TILE), BF16),
            ((TILE // CAP, CAP, tiles * TILE), BF16),
            ((row_tiles, TILE, tiles * TILE), BF16),
            ((row_tiles + blocks, TILE, tiles * TILE), BF16),
            ((CAP, tiles * TILE), i32),
            ((CAP, tiles * TILE), i32),
            ((halves, tiles * TILE, TILE), BF16),
            ((halves, reps, TILE, TILE), BF16),
            ((halves, reps, TILE, TILE), BF16),
            ((halves, TILE, TILE), F32),
            ((TILE, hidden), BF16),
            ((TILE, hidden), BF16),
            ((reps, TILE, TILE), BF16),
            ((reps, TILE, TILE), BF16),
            ((halves, doms, CAP, TILE), BF16),
            ((halves, doms, CAP, TILE), BF16),
            ((halves, row_tiles, TILE, TILE), F32),
            ((halves, reps, TILE, TILE), BF16),
            ((halves, reps, TILE, TILE), BF16),
            ((doms, chunk, TILE), F32),
            ((doms, chunk, TILE), F32),
            ((chunk, TILE), F32),
            ((reps, chunk, TILE), F32),
            ((doms // reps, chunk, TILE), F32),
        )
        return pl.pallas_call(
            functools.partial(kernel, doms, reps, float(rows * doms) ** (-0.5)),
            out_shape=out_shape,
            in_specs=[hbm] * 9,
            out_specs=(vmem,) * 3,
            scratch_shapes=[
                item[0](*item[1:]) if len(item) == 3 else pltpu.VMEM(*item) for item in scratch
            ]
            + [
                pltpu.SemaphoreType.DMA((9,)),
                pltpu.SemaphoreType.DMA((phases,)),
                pltpu.SemaphoreType.DMA((phases,)),
            ],
            compiler_params=pltpu.CompilerParams(
                collective_id=0, has_side_effects=True, vmem_limit_bytes=60 * 2**20
            ),
        )(
            features,
            weight,
            adjacency,
            jnp.swapaxes(send_rows, 2, 3),
            send_counts,
            tile_row,
            tile_column,
            tile_counts,
            cotangent,
        )

    in_specs = (
        P("dom", None),
        P(),
        P("dom", "rep", None, None, None),
        P("dom", "rep", None),
        P("dom", "rep", None),
        P("dom", "rep"),
        P("dom", "rep", None, None),
        P("dom", "rep", None),
        P(("dom", "rep"), None),
    )
    out_specs = (P(("dom", "rep"), None), P(("dom", "rep"), None), P("rep", None))
    return jax.shard_map(local, mesh=mesh, in_specs=in_specs, out_specs=out_specs, check_vma=False)
```

```python
import functools

import jax
import jax.numpy as jnp
from jax import lax
from jax.experimental import pallas as pl
from jax.experimental.pallas import tpu as pltpu
from jax.sharding import PartitionSpec as P

GELU_SCALE = 0.7978845608028654
GELU_CUBIC = 0.044715
MESH = pl.DeviceIdType.MESH
TILE = 128
CAP = 16
F32 = jnp.float32
BF16 = jnp.bfloat16


def gelu_pair(pre_act):
    inner_arg = GELU_SCALE * (pre_act + GELU_CUBIC * pre_act * pre_act * pre_act)
    tanh_part = jnp.tanh(inner_arg)
    activated = 0.5 * pre_act * (1.0 + tanh_part)
    derivative = 0.5 * (1.0 + tanh_part) + 0.5 * pre_act * (
        1.0 - tanh_part * tanh_part
    ) * GELU_SCALE * (1.0 + 3.0 * GELU_CUBIC * pre_act * pre_act)
    return (activated, derivative)


def loop(start, stop, body):
    def step(k, carry):
        body(k)
        return carry

    lax.fori_loop(start, stop, step, 0)


def kernel(
    doms,
    reps,
    scale,
    features_in,
    weight_in,
    adjacency_in,
    lists_in,
    list_counts_in,
    tile_row_in,
    tile_column_in,
    tile_count_in,
    cotangent_in,
    output,
    feature_grad,
    weight_grad,
    features,
    weight,
    adjacency,
    lists,
    list_counts,
    tile_row,
    tile_column,
    tile_count,
    cotangent,
    listed,
    space_low,
    space_high,
    outgoing,
    scatter,
    a_cat,
    at_cat,
    by_row,
    by_column,
    row_lanes,
    column_lanes,
    picked,
    agg_send,
    agg_recv,
    own_sum,
    aggregate,
    pre_grad,
    row_grads_low,
    row_grads_high,
    back_send,
    back_recv,
    feature_part,
    feat_send,
    feat_recv,
    w_send,
    w_recv,
    w_sum,
    w_rep,
    w_done,
    copy_sems,
    send_sems,
    recv_sems,
):
    d = lax.axis_index("dom")
    r = lax.axis_index("rep")
    rows, hidden = features.shape
    tiles = adjacency.shape[0]
    row_tiles = rows // TILE
    blocks = doms * CAP // TILE
    per = TILE // CAP
    first_halo = rows // CAP
    halves = hidden // TILE
    space = (space_low, space_high)
    row_grads = (row_grads_low, row_grads_high)
    HALO, AGG, GRAD, BACK, FEAT = (halves * k for k in range(5))
    W_DOM, W_REP, W_END, AGG_LAST = (halves * 5 + k for k in range(4))

    barrier = pltpu.get_barrier_semaphore()

    def greet_dom(k):
        pl.semaphore_signal(
            barrier, inc=1, device_id={"dom": lax.rem(d + k, doms)}, device_id_type=MESH
        )

    def greet_rep(k):
        pl.semaphore_signal(
            barrier, inc=1, device_id={"rep": lax.rem(r + k, reps)}, device_id_type=MESH
        )

    loads = [
        pltpu.make_async_copy(src, dst, copy_sems.at[k])
        for k, (src, dst) in enumerate(
            (
                (lists_in.at[0, 0], lists),
                (list_counts_in.at[0], list_counts),
                (features_in, features),
                (adjacency_in.at[0, 0], adjacency),
                (tile_row_in, tile_row),
                (tile_column_in, tile_column),
                (tile_count_in, tile_count),
                (weight_in, weight),
                (cotangent_in, cotangent),
            )
        )
    ]
    for load in loads[:3]:
        load.start()
    loop(doms // 2, doms, greet_dom)
    loop(1, doms // 2, greet_dom)
    loop(1, reps, greet_rep)
    for load in loads[3:]:
        load.start()

    def push(src, dst, phase, target):
        pltpu.make_async_remote_copy(
            src_ref=src,
            dst_ref=dst,
            send_sem=send_sems.at[phase],
            recv_sem=recv_sems.at[phase],
            device_id=target,
            device_id_type=MESH,
        ).start()

    def await_bytes(ref, sems, phase):
        pltpu.make_async_copy(ref, ref, sems.at[phase]).wait()

    def send_block(block, src, dst, phase):
        def send(j):
            q = block * per + j

            @pl.when(q != d)
            def _():
                push(src.at[q], dst, phase, {"dom": q})

        loop(0, per, send)

    def far_block(b):
        step = (2 * lax.rem(b, 2) - 1) * ((b + 1) // 2)
        return lax.rem(d // per + blocks // 2 + step + 2 * blocks, blocks)

    far_reps = sorted(range(1, reps), key=lambda k: -min(k, reps - k))

    def share_rows(h, k, c):
        size = TILE // 2
        mine = row_grads[h].at[r, c * size : (c + 1) * size]
        push(mine, mine, GRAD + h, {"rep": lax.rem(r + k, reps)})

    lane = lax.broadcasted_iota(jnp.int32, (TILE, TILE), 1)
    row = lax.broadcasted_iota(jnp.int32, (TILE, TILE), 0)
    for load in loads[:3]:
        load.wait()
    slot = lax.broadcasted_iota(jnp.int32, (CAP, doms), 0)
    live_lists = jnp.where(slot < list_counts[...], lists[...], -1)
    for p in range(doms):
        listed[p // per, p % per * CAP : (p % per + 1) * CAP, :] = jnp.broadcast_to(
            live_lists[:, p : p + 1], (CAP, TILE)
        )

    def gather(block):
        rows_of = listed[block]
        onehot = jnp.concatenate(
            [jnp.where(rows_of == lane + i * TILE, 1.0, 0.0).astype(BF16) for i in range(row_tiles)],
            axis=1,
        )
        found = jnp.dot(onehot, features[...], preferred_element_type=F32).astype(BF16)
        for h in range(halves):
            outgoing[h, pl.ds(block * per, per)] = found[:, h * TILE : (h + 1) * TILE].reshape(
                per, CAP, TILE
            )

    def send_halo(block, h):
        send_block(block, outgoing.at[h], space[h].at[first_halo + d], HALO + h)

    loop(0, blocks, gather)
    pl.semaphore_wait(barrier, doms + reps - 2)
    for h in range(halves):
        loop(0, blocks, lambda b: send_halo(far_block(b), h))

    for load in loads[3:]:
        load.wait()
    for t in range(tiles):
        lanes = slice(t * TILE, (t + 1) * TILE)
        live = t < tile_count[0, 0]
        row_lanes[:, lanes] = jnp.full(
            (CAP, TILE), jnp.where(live, tile_row[0, 0, t], -1), jnp.int32
        )
        column_lanes[:, lanes] = jnp.full(
            (CAP, TILE), jnp.where(live, tile_column[0, 0, t], -1), jnp.int32
        )
        a_cat[:, :, lanes] = adjacency[t].reshape(per, CAP, TILE)
        at_cat[:, :, lanes] = adjacency[t].T.reshape(per, CAP, TILE)

    def mask_tiles(dst, values, lanes):
        def one(i):
            mask = jnp.where(lanes[...] == i, 1.0, 0.0).astype(BF16)
            dst[i] = (values[...] * mask[None]).reshape(TILE, tiles * TILE)

        loop(0, dst.shape[0], one)

    mask_tiles(by_row, a_cat, row_lanes)
    for h in range(halves):
        space[h][pl.ds(0, first_halo)] = features[:, h * TILE : (h + 1) * TILE].reshape(
            first_halo, CAP, TILE
        )
        space[h][first_halo + d] = jnp.zeros((CAP, TILE), BF16)
        back_recv[h, d] = jnp.zeros((CAP, TILE), BF16)
    mask_tiles(by_column, at_cat, column_lanes)

    def make_scatter(block):
        rows_of = listed[block].T
        for i in range(row_tiles):
            scatter[i, block] = jnp.where(rows_of == row + i * TILE, 1.0, 0.0).astype(BF16)

    loop(0, blocks, make_scatter)

    def tile_sum(values, h):
        return jnp.dot(values, picked[h], preferred_element_type=F32)

    pieces = 2
    piece_rows = TILE // pieces
    piece_at = [slice(c * piece_rows, (c + 1) * piece_rows) for c in range(pieces)]
    last = halves - 1

    def send_piece(h, i, c):
        push(
            agg_send.at[h, i, piece_at[c]],
            agg_recv.at[h, r, piece_at[c]],
            AGG_LAST + c if h == last else AGG + h,
            {"rep": i},
        )

    for h in range(halves):
        await_bytes(space[h].at[pl.ds(first_halo, doms - 1)], recv_sems, HALO + h)
        for t in range(tiles):
            picked[h, t * TILE : (t + 1) * TILE, :] = space[h][
                pl.ds(tile_column[0, 0, t] * per, per)
            ].reshape(TILE, TILE)
        for k in far_reps:
            i = lax.rem(r + k, reps)
            agg_send[h, i] = tile_sum(by_row[i], h).astype(BF16)
            if h == last:
                send_piece(h, i, 0)
            else:
                push(agg_send.at[h, i], agg_recv.at[h, r], AGG + h, {"rep": i})
        if h == last:
            for c in range(1, pieces):
                for k in far_reps:
                    send_piece(h, lax.rem(r + k, reps), c)
        own_sum[h] = tile_sum(by_row[r], h)

    for h in range(last):
        await_bytes(agg_recv.at[h, pl.ds(0, reps - 1)], recv_sems, AGG + h)
        for k in range(1, reps):
            own_sum[h] += agg_recv[h, lax.rem(r + k, reps)].astype(F32)
    for c in range(pieces):
        await_bytes(agg_recv.at[last, pl.ds(0, reps - 1), piece_at[c]], recv_sems, AGG_LAST + c)
        total = own_sum[last, piece_at[c]]
        for k in range(1, reps):
            total = total + agg_recv[last, lax.rem(r + k, reps), piece_at[c]].astype(F32)
        piece = jnp.concatenate(
            [own_sum[h, piece_at[c]].astype(BF16) for h in range(last)] + [total.astype(BF16)],
            axis=1,
        )
        aggregate[piece_at[c]] = piece
        pre_act = lax.dot_general(
            piece, weight[...], (((1,), (1,)), ((), ())), preferred_element_type=F32
        )
        activated, derivative = gelu_pair(pre_act)
        grad = (cotangent[piece_at[c]].astype(F32) * derivative).astype(BF16)
        pre_grad[piece_at[c]] = grad
        output[piece_at[c]] = activated.astype(BF16)
        row_grad = jnp.dot(grad, weight[...], preferred_element_type=F32).astype(BF16)
        for h in range(halves):
            row_grads[h][r, piece_at[c]] = row_grad[:, h * TILE : (h + 1) * TILE]
        for k in far_reps:
            share_rows(0, k, c)
    for h in range(1, halves):
        for c in range(pieces):
            for k in far_reps:
                share_rows(h, k, c)

    w_part = lax.dot_general(
        pre_grad[...], aggregate[...], (((0,), (0,)), ((), ())), preferred_element_type=F32
    )
    chunk = w_send.shape[1]
    half = doms // 2
    for h in range(2):
        w_send[h * half : (h + 1) * half] = w_part[:, h * TILE : (h + 1) * TILE].reshape(
            half, chunk, TILE
        )
    loop(0, blocks, lambda b: send_block(far_block(b), w_send, w_recv.at[d], W_DOM))
    w_recv[d] = w_send[d]

    for h in range(halves):
        await_bytes(row_grads[h].at[pl.ds(0, reps - 1)], recv_sems, GRAD + h)
        for t in range(tiles):
            picked[h, t * TILE : (t + 1) * TILE, :] = row_grads[h][tile_row[0, 0, t]]

        def backward_halo(b):
            block = far_block(b)
            grads = tile_sum(by_column[block + row_tiles], h).astype(BF16)
            back_send[h, pl.ds(block * per, per)] = grads.reshape(per, CAP, TILE)
            send_block(block, back_send.at[h], back_recv.at[h, d], BACK + h)

        loop(0, blocks, backward_halo)

        def backward_local(i):
            pair = by_column[pl.ds(2 * i, 2)].reshape(2 * TILE, tiles * TILE)
            feature_part[h, pl.ds(2 * i, 2)] = tile_sum(pair, h).reshape(2, TILE, TILE)

        loop(0, row_tiles // 2, backward_local)

    spread = half // reps
    holder = lax.rem(d, half) // spread
    place = (d // half) * spread + lax.rem(d, spread)
    await_bytes(w_recv.at[pl.ds(0, doms - 1)], recv_sems, W_DOM)
    w_sum[...] = jnp.sum(w_recv[...], axis=0)

    @pl.when(r != holder)
    def _():
        push(w_sum, w_rep.at[r], W_REP, {"rep": holder})

    def finish_weight():
        @pl.when(r == holder)
        def _():
            await_bytes(w_rep.at[pl.ds(0, reps - 1)], recv_sems, W_REP)
            whole = w_sum[...]
            for k in range(1, reps):
                whole = whole + w_rep[lax.rem(r + k, reps)]
            w_done[place] = whole * scale

            def share_done(k):
                push(w_done.at[place], w_done.at[place], W_END, {"dom": lax.rem(d + k, doms)})

            loop(1, doms, share_done)

    own = []
    for h in range(halves):
        await_bytes(back_recv.at[h, pl.ds(0, doms - 1)], recv_sems, BACK + h)

        def feature_rows(i):
            total = feature_part[h, i]
            for block in range(blocks):
                returned = back_recv[h, block * per : (block + 1) * per].reshape(TILE, TILE)
                total = total + jnp.dot(scatter[i, block], returned, preferred_element_type=F32)
            return total

        for k in far_reps:
            i = lax.rem(r + k, reps)
            feat_send[h, i] = feature_rows(i).astype(BF16)
            push(feat_send.at[h, i], feat_recv.at[h, r], FEAT + h, {"rep": i})
        own.append(feature_rows(r))
        if h == 0:
            finish_weight()

    @pl.when(r == holder)
    def _():
        await_bytes(w_done.at[pl.ds(0, 2 * spread - 1)], recv_sems, W_END)

    @pl.when(r != holder)
    def _():
        await_bytes(w_done, recv_sems, W_END)

    for h in range(2):
        weight_grad[:, h * TILE : (h + 1) * TILE] = w_done[h * spread : (h + 1) * spread].reshape(
            spread * chunk, TILE
        )
    for h in range(halves):
        await_bytes(feat_recv.at[h, pl.ds(0, reps - 1)], recv_sems, FEAT + h)
        total = own[h]
        for k in range(1, reps):
            total = total + feat_recv[h, lax.rem(r + k, reps)].astype(F32)
        feature_grad[:, h * TILE : (h + 1) * TILE] = total.astype(BF16)

    for h in range(halves):
        await_bytes(outgoing.at[h, pl.ds(0, doms - 1)], send_sems, HALO + h)
        if h != last:
            await_bytes(agg_send.at[h, pl.ds(0, reps - 1)], send_sems, AGG + h)
        await_bytes(row_grads[h].at[pl.ds(0, reps - 1)], send_sems, GRAD + h)
        await_bytes(back_send.at[h, pl.ds(0, doms - 1)], send_sems, BACK + h)
        await_bytes(feat_send.at[h, pl.ds(0, reps - 1)], send_sems, FEAT + h)
    for c in range(pieces):
        await_bytes(agg_send.at[last, pl.ds(0, reps - 1), piece_at[c]], send_sems, AGG_LAST + c)
    await_bytes(w_send.at[pl.ds(0, doms - 1)], send_sems, W_DOM)

    @pl.when(r != holder)
    def _():
        await_bytes(w_sum, send_sems, W_REP)

    @pl.when(r == holder)
    def _():
        await_bytes(w_send.at[pl.ds(0, doms - 1)], send_sems, W_END)


def solution(mesh):
    doms, reps = mesh.shape["dom"], mesh.shape["rep"]

    def local(
        features,
        weight,
        adjacency,
        tile_row,
        tile_column,
        tile_counts,
        send_rows,
        send_counts,
        cotangent,
    ):
        rows, hidden = features.shape
        tiles = adjacency.shape[2]
        row_tiles = rows // TILE
        blocks = doms * CAP // TILE
        halves = hidden // TILE
        chunk = 2 * hidden // doms
        vmem = pl.BlockSpec(memory_space=pltpu.VMEM)
        hbm = pl.BlockSpec(memory_space=pltpu.HBM)
        i32 = jnp.int32
        phases = halves * 5 + 5
        out_shape = (
            jax.ShapeDtypeStruct((rows // reps, hidden), BF16),
            jax.ShapeDtypeStruct((rows // reps, hidden), BF16),
            jax.ShapeDtypeStruct((hidden // reps, hidden), F32),
        )
        scratch = (
            ((rows, hidden), BF16),
            ((hidden, hidden), BF16),
            ((tiles, TILE, TILE), BF16),
            ((CAP, doms), i32),
            ((1, doms), i32),
            (pltpu.SMEM, (1, 1, tiles), i32),
            (pltpu.SMEM, (1, 1, tiles), i32),
            (pltpu.SMEM, (1, 1), i32),
            ((rows // reps, hidden), BF16),
            ((blocks, TILE, TILE), i32),
            ((rows // CAP + doms, CAP, TILE), BF16),
            ((rows // CAP + doms, CAP, TILE), BF16),
            ((halves, doms, CAP, TILE), BF16),
            ((row_tiles, blocks, TILE, TILE), BF16),
            ((TILE // CAP, CAP, tiles * TILE), BF16),
            ((TILE // CAP, CAP, tiles * TILE), BF16),
            ((row_tiles, TILE, tiles * TILE), BF16),
            ((row_tiles + blocks, TILE, tiles * TILE), BF16),
            ((CAP, tiles * TILE), i32),
            ((CAP, tiles * TILE), i32),
            ((halves, tiles * TILE, TILE), BF16),
            ((halves, reps, TILE, TILE), BF16),
            ((halves, reps, TILE, TILE), BF16),
            ((halves, TILE, TILE), F32),
            ((TILE, hidden), BF16),
            ((TILE, hidden), BF16),
            ((reps, TILE, TILE), BF16),
            ((reps, TILE, TILE), BF16),
            ((halves, doms, CAP, TILE), BF16),
            ((halves, doms, CAP, TILE), BF16),
            ((halves, row_tiles, TILE, TILE), F32),
            ((halves, reps, TILE, TILE), BF16),
            ((halves, reps, TILE, TILE), BF16),
            ((doms, chunk, TILE), F32),
            ((doms, chunk, TILE), F32),
            ((chunk, TILE), F32),
            ((reps, chunk, TILE), F32),
            ((doms // reps, chunk, TILE), F32),
        )
        return pl.pallas_call(
            functools.partial(kernel, doms, reps, float(rows * doms) ** (-0.5)),
            out_shape=out_shape,
            in_specs=[hbm] * 9,
            out_specs=(vmem,) * 3,
            scratch_shapes=[
                item[0](*item[1:]) if len(item) == 3 else pltpu.VMEM(*item) for item in scratch
            ]
            + [
                pltpu.SemaphoreType.DMA((9,)),
                pltpu.SemaphoreType.DMA((phases,)),
                pltpu.SemaphoreType.DMA((phases,)),
            ],
            compiler_params=pltpu.CompilerParams(
                collective_id=0, has_side_effects=True, vmem_limit_bytes=60 * 2**20
            ),
        )(
            features,
            weight,
            adjacency,
            jnp.swapaxes(send_rows, 2, 3),
            send_counts,
            tile_row,
            tile_column,
            tile_counts,
            cotangent,
        )

    in_specs = (
        P("dom", None),
        P(),
        P("dom", "rep", None, None, None),
        P("dom", "rep", None),
        P("dom", "rep", None),
        P("dom", "rep"),
        P("dom", "rep", None, None),
        P("dom", "rep", None),
        P(("dom", "rep"), None),
    )
    out_specs = (P(("dom", "rep"), None), P(("dom", "rep"), None), P("rep", None))
    return jax.shard_map(local, mesh=mesh, in_specs=in_specs, out_specs=out_specs, check_vma=False)
```

```python
import functools

import jax
import jax.numpy as jnp
from jax import lax
from jax.experimental import pallas as pl
from jax.experimental.pallas import tpu as pltpu
from jax.sharding import PartitionSpec as P

GELU_SCALE = 0.7978845608028654
GELU_CUBIC = 0.044715
MESH = pl.DeviceIdType.MESH
TILE = 128
CAP = 16
F32 = jnp.float32
BF16 = jnp.bfloat16


def gelu_pair(pre_act):
    inner_arg = GELU_SCALE * (pre_act + GELU_CUBIC * pre_act * pre_act * pre_act)
    tanh_part = jnp.tanh(inner_arg)
    activated = 0.5 * pre_act * (1.0 + tanh_part)
    derivative = 0.5 * (1.0 + tanh_part) + 0.5 * pre_act * (
        1.0 - tanh_part * tanh_part
    ) * GELU_SCALE * (1.0 + 3.0 * GELU_CUBIC * pre_act * pre_act)
    return (activated, derivative)


def loop(start, stop, body):
    def step(k, carry):
        body(k)
        return carry

    lax.fori_loop(start, stop, step, 0)


def kernel(
    doms,
    reps,
    scale,
    features_in,
    weight_in,
    adjacency_in,
    lists_in,
    list_counts_in,
    tile_row_in,
    tile_column_in,
    tile_count_in,
    cotangent_in,
    output_out,
    feature_grad_out,
    weight_grad_out,
    output,
    feature_grad,
    weight_grad,
    features,
    weight,
    adjacency,
    lists,
    list_counts,
    tile_row,
    tile_column,
    tile_count,
    cotangent,
    listed,
    space_low,
    space_high,
    outgoing,
    scatter,
    a_cat,
    at_cat,
    by_row,
    by_column,
    row_lanes,
    column_lanes,
    picked,
    agg_send,
    agg_recv,
    own_sum,
    aggregate,
    pre_grad,
    row_grads_low,
    row_grads_high,
    back_send,
    back_recv,
    feature_part,
    feat_send,
    feat_recv,
    w_send,
    w_recv,
    w_sum,
    w_rep,
    w_done,
    copy_sems,
    send_sems,
    recv_sems,
):
    d = lax.axis_index("dom")
    r = lax.axis_index("rep")
    rows, hidden = features.shape
    tiles = adjacency.shape[0]
    row_tiles = rows // TILE
    blocks = doms * CAP // TILE
    per = TILE // CAP
    first_halo = rows // CAP
    halves = hidden // TILE
    space = (space_low, space_high)
    row_grads = (row_grads_low, row_grads_high)
    HALO, AGG, GRAD, BACK, FEAT = (halves * k for k in range(5))
    W_DOM, W_REP, W_END, AGG_LAST = (halves * 5 + k for k in range(4))

    barrier = pltpu.get_barrier_semaphore()

    def greet_dom(k):
        pl.semaphore_signal(
            barrier, inc=1, device_id={"dom": lax.rem(d + k, doms)}, device_id_type=MESH
        )

    def greet_rep(k):
        pl.semaphore_signal(
            barrier, inc=1, device_id={"rep": lax.rem(r + k, reps)}, device_id_type=MESH
        )

    loads = [
        pltpu.make_async_copy(src, dst, copy_sems.at[k])
        for k, (src, dst) in enumerate(
            (
                (lists_in.at[0, 0], lists),
                (list_counts_in.at[0], list_counts),
                (features_in, features),
                (adjacency_in.at[0, 0], adjacency),
                (tile_row_in, tile_row),
                (tile_column_in, tile_column),
                (tile_count_in, tile_count),
                (weight_in, weight),
                (cotangent_in, cotangent),
            )
        )
    ]
    for load in loads[:3]:
        load.start()
    loop(doms // 2, doms, greet_dom)
    loop(1, doms // 2, greet_dom)
    loop(1, reps, greet_rep)
    for load in loads[3:]:
        load.start()

    def push(src, dst, phase, target):
        pltpu.make_async_remote_copy(
            src_ref=src,
            dst_ref=dst,
            send_sem=send_sems.at[phase],
            recv_sem=recv_sems.at[phase],
            device_id=target,
            device_id_type=MESH,
        ).start()

    def await_bytes(ref, sems, phase):
        pltpu.make_async_copy(ref, ref, sems.at[phase]).wait()

    def send_block(block, src, dst, phase):
        def send(j):
            q = block * per + j

            @pl.when(q != d)
            def _():
                push(src.at[q], dst, phase, {"dom": q})

        loop(0, per, send)

    def far_block(b):
        step = (2 * lax.rem(b, 2) - 1) * ((b + 1) // 2)
        return lax.rem(d // per + blocks // 2 + step + 2 * blocks, blocks)

    far_reps = sorted(range(1, reps), key=lambda k: -min(k, reps - k))

    def share_rows(h, k, c):
        size = TILE // 2
        mine = row_grads[h].at[r, c * size : (c + 1) * size]
        push(mine, mine, GRAD + h, {"rep": lax.rem(r + k, reps)})

    lane = lax.broadcasted_iota(jnp.int32, (TILE, TILE), 1)
    row = lax.broadcasted_iota(jnp.int32, (TILE, TILE), 0)
    for load in loads[:3]:
        load.wait()
    slot = lax.broadcasted_iota(jnp.int32, (CAP, doms), 0)
    live_lists = jnp.where(slot < list_counts[...], lists[...], -1)
    for p in range(doms):
        listed[p // per, p % per * CAP : (p % per + 1) * CAP, :] = jnp.broadcast_to(
            live_lists[:, p : p + 1], (CAP, TILE)
        )

    def gather(block):
        rows_of = listed[block]
        onehot = jnp.concatenate(
            [jnp.where(rows_of == lane + i * TILE, 1.0, 0.0).astype(BF16) for i in range(row_tiles)],
            axis=1,
        )
        found = jnp.dot(onehot, features[...], preferred_element_type=F32).astype(BF16)
        for h in range(halves):
            outgoing[h, pl.ds(block * per, per)] = found[:, h * TILE : (h + 1) * TILE].reshape(
                per, CAP, TILE
            )

    def send_halo(block, h):
        send_block(block, outgoing.at[h], space[h].at[first_halo + d], HALO + h)

    loop(0, blocks, gather)
    pl.semaphore_wait(barrier, doms + reps - 2)
    for h in range(halves):
        loop(0, blocks, lambda b: send_halo(far_block(b), h))

    for load in loads[3:]:
        load.wait()
    for t in range(tiles):
        lanes = slice(t * TILE, (t + 1) * TILE)
        live = t < tile_count[0, 0]
        row_lanes[:, lanes] = jnp.full(
            (CAP, TILE), jnp.where(live, tile_row[0, 0, t], -1), jnp.int32
        )
        column_lanes[:, lanes] = jnp.full(
            (CAP, TILE), jnp.where(live, tile_column[0, 0, t], -1), jnp.int32
        )
        a_cat[:, :, lanes] = adjacency[t].reshape(per, CAP, TILE)
        at_cat[:, :, lanes] = adjacency[t].T.reshape(per, CAP, TILE)

    def mask_tiles(dst, values, lanes):
        def one(i):
            mask = jnp.where(lanes[...] == i, 1.0, 0.0).astype(BF16)
            dst[i] = (values[...] * mask[None]).reshape(TILE, tiles * TILE)

        loop(0, dst.shape[0], one)

    mask_tiles(by_row, a_cat, row_lanes)
    for h in range(halves):
        space[h][pl.ds(0, first_halo)] = features[:, h * TILE : (h + 1) * TILE].reshape(
            first_halo, CAP, TILE
        )
        space[h][first_halo + d] = jnp.zeros((CAP, TILE), BF16)
        back_recv[h, d] = jnp.zeros((CAP, TILE), BF16)
    mask_tiles(by_column, at_cat, column_lanes)

    def make_scatter(block):
        rows_of = listed[block].T
        for i in range(row_tiles):
            scatter[i, block] = jnp.where(rows_of == row + i * TILE, 1.0, 0.0).astype(BF16)

    loop(0, blocks, make_scatter)

    def tile_sum(values, h):
        return jnp.dot(values, picked[h], preferred_element_type=F32)

    pieces = 2
    piece_rows = TILE // pieces
    piece_at = [slice(c * piece_rows, (c + 1) * piece_rows) for c in range(pieces)]
    last = halves - 1

    def send_piece(h, i, c):
        push(
            agg_send.at[h, i, piece_at[c]],
            agg_recv.at[h, r, piece_at[c]],
            AGG_LAST + c if h == last else AGG + h,
            {"rep": i},
        )

    for h in range(halves):
        await_bytes(space[h].at[pl.ds(first_halo, doms - 1)], recv_sems, HALO + h)
        for t in range(tiles):
            picked[h, t * TILE : (t + 1) * TILE, :] = space[h][
                pl.ds(tile_column[0, 0, t] * per, per)
            ].reshape(TILE, TILE)
        for k in far_reps:
            i = lax.rem(r + k, reps)
            agg_send[h, i] = tile_sum(by_row[i], h).astype(BF16)
            if h == last:
                send_piece(h, i, 0)
            else:
                push(agg_send.at[h, i], agg_recv.at[h, r], AGG + h, {"rep": i})
        if h == last:
            for c in range(1, pieces):
                for k in far_reps:
                    send_piece(h, lax.rem(r + k, reps), c)
        own_sum[h] = tile_sum(by_row[r], h)

    for h in range(last):
        await_bytes(agg_recv.at[h, pl.ds(0, reps - 1)], recv_sems, AGG + h)
        for k in range(1, reps):
            own_sum[h] += agg_recv[h, lax.rem(r + k, reps)].astype(F32)
    for c in range(pieces):
        await_bytes(agg_recv.at[last, pl.ds(0, reps - 1), piece_at[c]], recv_sems, AGG_LAST + c)
        total = own_sum[last, piece_at[c]]
        for k in range(1, reps):
            total = total + agg_recv[last, lax.rem(r + k, reps), piece_at[c]].astype(F32)
        piece = jnp.concatenate(
            [own_sum[h, piece_at[c]].astype(BF16) for h in range(last)] + [total.astype(BF16)],
            axis=1,
        )
        aggregate[piece_at[c]] = piece
        pre_act = lax.dot_general(
            piece, weight[...], (((1,), (1,)), ((), ())), preferred_element_type=F32
        )
        activated, derivative = gelu_pair(pre_act)
        grad = (cotangent[piece_at[c]].astype(F32) * derivative).astype(BF16)
        pre_grad[piece_at[c]] = grad
        output[piece_at[c]] = activated.astype(BF16)
        row_grad = jnp.dot(grad, weight[...], preferred_element_type=F32).astype(BF16)
        for h in range(halves):
            row_grads[h][r, piece_at[c]] = row_grad[:, h * TILE : (h + 1) * TILE]
        for k in far_reps:
            share_rows(0, k, c)
    for h in range(1, halves):
        for c in range(pieces):
            for k in far_reps:
                share_rows(h, k, c)

    stores = [
        pltpu.make_async_copy(src, dst, copy_sems.at[len(loads) + k])
        for k, (src, dst) in enumerate(
            ((output, output_out), (weight_grad, weight_grad_out), (feature_grad, feature_grad_out))
        )
    ]
    stores[0].start()

    w_part = lax.dot_general(
        pre_grad[...], aggregate[...], (((0,), (0,)), ((), ())), preferred_element_type=F32
    )
    chunk = w_send.shape[1]
    half = doms // 2
    for h in range(2):
        w_send[h * half : (h + 1) * half] = w_part[:, h * TILE : (h + 1) * TILE].reshape(
            half, chunk, TILE
        )
    loop(0, blocks, lambda b: send_block(far_block(b), w_send, w_recv.at[d], W_DOM))
    w_recv[d] = w_send[d]

    for h in range(halves):
        await_bytes(row_grads[h].at[pl.ds(0, reps - 1)], recv_sems, GRAD + h)
        for t in range(tiles):
            picked[h, t * TILE : (t + 1) * TILE, :] = row_grads[h][tile_row[0, 0, t]]

        def backward_halo(b):
            block = far_block(b)
            grads = tile_sum(by_column[block + row_tiles], h).astype(BF16)
            back_send[h, pl.ds(block * per, per)] = grads.reshape(per, CAP, TILE)
            send_block(block, back_send.at[h], back_recv.at[h, d], BACK + h)

        loop(0, blocks, backward_halo)

        def backward_local(i):
            pair = by_column[pl.ds(2 * i, 2)].reshape(2 * TILE, tiles * TILE)
            feature_part[h, pl.ds(2 * i, 2)] = tile_sum(pair, h).reshape(2, TILE, TILE)

        loop(0, row_tiles // 2, backward_local)

    spread = half // reps
    holder = lax.rem(d, half) // spread
    place = (d // half) * spread + lax.rem(d, spread)
    await_bytes(w_recv.at[pl.ds(0, doms - 1)], recv_sems, W_DOM)
    w_sum[...] = jnp.sum(w_recv[...], axis=0)

    @pl.when(r != holder)
    def _():
        push(w_sum, w_rep.at[r], W_REP, {"rep": holder})

    def finish_weight():
        @pl.when(r == holder)
        def _():
            await_bytes(w_rep.at[pl.ds(0, reps - 1)], recv_sems, W_REP)
            whole = w_sum[...]
            for k in range(1, reps):
                whole = whole + w_rep[lax.rem(r + k, reps)]
            w_done[place] = whole * scale

            def share_done(k):
                push(w_done.at[place], w_done.at[place], W_END, {"dom": lax.rem(d + k, doms)})

            loop(1, doms, share_done)

    own = []
    for h in range(halves):
        await_bytes(back_recv.at[h, pl.ds(0, doms - 1)], recv_sems, BACK + h)

        def feature_rows(i):
            total = feature_part[h, i]
            for block in range(blocks):
                returned = back_recv[h, block * per : (block + 1) * per].reshape(TILE, TILE)
                total = total + jnp.dot(scatter[i, block], returned, preferred_element_type=F32)
            return total

        for k in far_reps:
            i = lax.rem(r + k, reps)
            feat_send[h, i] = feature_rows(i).astype(BF16)
            push(feat_send.at[h, i], feat_recv.at[h, r], FEAT + h, {"rep": i})
        own.append(feature_rows(r))
        if h == 0:
            finish_weight()

    @pl.when(r == holder)
    def _():
        await_bytes(w_done.at[pl.ds(0, 2 * spread - 1)], recv_sems, W_END)

    @pl.when(r != holder)
    def _():
        await_bytes(w_done, recv_sems, W_END)

    for h in range(2):
        weight_grad[:, h * TILE : (h + 1) * TILE] = w_done[h * spread : (h + 1) * spread].reshape(
            spread * chunk, TILE
        )
    stores[1].start()
    for h in range(halves):
        await_bytes(feat_recv.at[h, pl.ds(0, reps - 1)], recv_sems, FEAT + h)
        total = own[h]
        for k in range(1, reps):
            total = total + feat_recv[h, lax.rem(r + k, reps)].astype(F32)
        feature_grad[:, h * TILE : (h + 1) * TILE] = total.astype(BF16)

    stores[2].start()

    for h in range(halves):
        await_bytes(outgoing.at[h, pl.ds(0, doms - 1)], send_sems, HALO + h)
        if h != last:
            await_bytes(agg_send.at[h, pl.ds(0, reps - 1)], send_sems, AGG + h)
        await_bytes(row_grads[h].at[pl.ds(0, reps - 1)], send_sems, GRAD + h)
        await_bytes(back_send.at[h, pl.ds(0, doms - 1)], send_sems, BACK + h)
        await_bytes(feat_send.at[h, pl.ds(0, reps - 1)], send_sems, FEAT + h)
    for c in range(pieces):
        await_bytes(agg_send.at[last, pl.ds(0, reps - 1), piece_at[c]], send_sems, AGG_LAST + c)
    await_bytes(w_send.at[pl.ds(0, doms - 1)], send_sems, W_DOM)

    @pl.when(r != holder)
    def _():
        await_bytes(w_sum, send_sems, W_REP)

    @pl.when(r == holder)
    def _():
        await_bytes(w_send.at[pl.ds(0, doms - 1)], send_sems, W_END)

    for store in stores:
        store.wait()


def hand_over(*refs):
    made, results, held, sems = refs[:3], refs[3:6], refs[6:9], refs[9]
    loads = [pltpu.make_async_copy(made[k], held[k], sems.at[k]) for k in range(3)]
    stores = [pltpu.make_async_copy(held[k], results[k], sems.at[3 + k]) for k in range(3)]
    for load in loads:
        load.start()
    for load, store in zip(loads, stores):
        load.wait()
        store.start()
    for store in stores:
        store.wait()


def solution(mesh):
    doms, reps = mesh.shape["dom"], mesh.shape["rep"]

    def local(
        features,
        weight,
        adjacency,
        tile_row,
        tile_column,
        tile_counts,
        send_rows,
        send_counts,
        cotangent,
    ):
        rows, hidden = features.shape
        tiles = adjacency.shape[2]
        row_tiles = rows // TILE
        blocks = doms * CAP // TILE
        halves = hidden // TILE
        chunk = 2 * hidden // doms
        hbm = pl.BlockSpec(memory_space=pltpu.HBM)
        i32 = jnp.int32
        phases = halves * 5 + 5
        out_shape = (
            jax.ShapeDtypeStruct((rows // reps, hidden), BF16),
            jax.ShapeDtypeStruct((rows // reps, hidden), BF16),
            jax.ShapeDtypeStruct((hidden // reps, hidden), F32),
        )
        staged = [pltpu.VMEM(leaf.shape, leaf.dtype) for leaf in out_shape]
        scratch = (
            ((rows, hidden), BF16),
            ((hidden, hidden), BF16),
            ((tiles, TILE, TILE), BF16),
            ((CAP, doms), i32),
            ((1, doms), i32),
            (pltpu.SMEM, (1, 1, tiles), i32),
            (pltpu.SMEM, (1, 1, tiles), i32),
            (pltpu.SMEM, (1, 1), i32),
            ((rows // reps, hidden), BF16),
            ((blocks, TILE, TILE), i32),
            ((rows // CAP + doms, CAP, TILE), BF16),
            ((rows // CAP + doms, CAP, TILE), BF16),
            ((halves, doms, CAP, TILE), BF16),
            ((row_tiles, blocks, TILE, TILE), BF16),
            ((TILE // CAP, CAP, tiles * TILE), BF16),
            ((TILE // CAP, CAP, tiles * TILE), BF16),
            ((row_tiles, TILE, tiles * TILE), BF16),
            ((row_tiles + blocks, TILE, tiles * TILE), BF16),
            ((CAP, tiles * TILE), i32),
            ((CAP, tiles * TILE), i32),
            ((halves, tiles * TILE, TILE), BF16),
            ((halves, reps, TILE, TILE), BF16),
            ((halves, reps, TILE, TILE), BF16),
            ((halves, TILE, TILE), F32),
            ((TILE, hidden), BF16),
            ((TILE, hidden), BF16),
            ((reps, TILE, TILE), BF16),
            ((reps, TILE, TILE), BF16),
            ((halves, doms, CAP, TILE), BF16),
            ((halves, doms, CAP, TILE), BF16),
            ((halves, row_tiles, TILE, TILE), F32),
            ((halves, reps, TILE, TILE), BF16),
            ((halves, reps, TILE, TILE), BF16),
            ((doms, chunk, TILE), F32),
            ((doms, chunk, TILE), F32),
            ((chunk, TILE), F32),
            ((reps, chunk, TILE), F32),
            ((doms // reps, chunk, TILE), F32),
        )
        made = pl.pallas_call(
            functools.partial(kernel, doms, reps, float(rows * doms) ** (-0.5)),
            out_shape=out_shape,
            in_specs=[hbm] * 9,
            out_specs=(hbm,) * 3,
            scratch_shapes=staged
            + [
                item[0](*item[1:]) if len(item) == 3 else pltpu.VMEM(*item) for item in scratch
            ]
            + [
                pltpu.SemaphoreType.DMA((12,)),
                pltpu.SemaphoreType.DMA((phases,)),
                pltpu.SemaphoreType.DMA((phases,)),
            ],
            compiler_params=pltpu.CompilerParams(
                collective_id=0, has_side_effects=True, vmem_limit_bytes=60 * 2**20
            ),
        )(
            features,
            weight,
            adjacency,
            jnp.swapaxes(send_rows, 2, 3),
            send_counts,
            tile_row,
            tile_column,
            tile_counts,
            cotangent,
        )
        return pl.pallas_call(
            hand_over,
            out_shape=out_shape,
            in_specs=[hbm] * 3,
            out_specs=(hbm,) * 3,
            scratch_shapes=staged + [pltpu.SemaphoreType.DMA((6,))],
            compiler_params=pltpu.CompilerParams(vmem_limit_bytes=60 * 2**20),
        )(*made)

    in_specs = (
        P("dom", None),
        P(),
        P("dom", "rep", None, None, None),
        P("dom", "rep", None),
        P("dom", "rep", None),
        P("dom", "rep"),
        P("dom", "rep", None, None),
        P("dom", "rep", None),
        P(("dom", "rep"), None),
    )
    out_specs = (P(("dom", "rep"), None), P(("dom", "rep"), None), P("rep", None))
    return jax.shard_map(local, mesh=mesh, in_specs=in_specs, out_specs=out_specs, check_vma=False)
```

```python
import functools

import jax
import jax.numpy as jnp
from jax import lax
from jax.experimental import pallas as pl
from jax.experimental.pallas import tpu as pltpu
from jax.sharding import PartitionSpec as P

GELU_SCALE = 0.7978845608028654
GELU_CUBIC = 0.044715
MESH = pl.DeviceIdType.MESH
TILE = 128
CAP = 16
F32 = jnp.float32
BF16 = jnp.bfloat16


def gelu_pair(pre_act):
    inner_arg = GELU_SCALE * (pre_act + GELU_CUBIC * pre_act * pre_act * pre_act)
    tanh_part = jnp.tanh(inner_arg)
    activated = 0.5 * pre_act * (1.0 + tanh_part)
    derivative = 0.5 * (1.0 + tanh_part) + 0.5 * pre_act * (
        1.0 - tanh_part * tanh_part
    ) * GELU_SCALE * (1.0 + 3.0 * GELU_CUBIC * pre_act * pre_act)
    return (activated, derivative)


def loop(start, stop, body):
    def step(k, carry):
        body(k)
        return carry

    lax.fori_loop(start, stop, step, 0)


def kernel(
    doms,
    reps,
    scale,
    features_in,
    weight_in,
    adjacency_in,
    lists_in,
    list_counts_in,
    tile_row_in,
    tile_column_in,
    tile_count_in,
    cotangent_in,
    output_out,
    feature_grad_out,
    weight_grad_out,
    output,
    feature_grad,
    weight_grad,
    features,
    weight,
    adjacency,
    lists,
    list_counts,
    tile_row,
    tile_column,
    tile_count,
    cotangent,
    listed,
    space_low,
    space_high,
    outgoing,
    scatter,
    a_cat,
    at_cat,
    by_row,
    by_column,
    row_lanes,
    column_lanes,
    picked,
    agg_send,
    agg_recv,
    own_sum,
    aggregate,
    pre_grad,
    row_grads_low,
    row_grads_high,
    back_send,
    back_recv,
    feature_part,
    feat_send,
    feat_recv,
    w_send,
    w_recv,
    w_sum,
    w_rep,
    w_done,
    copy_sems,
    send_sems,
    recv_sems,
):
    d = lax.axis_index("dom")
    r = lax.axis_index("rep")
    rows, hidden = features.shape
    tiles = adjacency.shape[0]
    row_tiles = rows // TILE
    blocks = doms * CAP // TILE
    per = TILE // CAP
    first_halo = rows // CAP
    halves = hidden // TILE
    space = (space_low, space_high)
    row_grads = (row_grads_low, row_grads_high)
    HALO, AGG, GRAD, BACK, FEAT = (halves * k for k in range(5))
    W_DOM, W_REP, W_END, AGG_LAST = (halves * 5 + k for k in range(4))

    barrier = pltpu.get_barrier_semaphore()

    def greet_dom(k):
        pl.semaphore_signal(
            barrier, inc=1, device_id={"dom": lax.rem(d + k, doms)}, device_id_type=MESH
        )

    def greet_rep(k):
        pl.semaphore_signal(
            barrier, inc=1, device_id={"rep": lax.rem(r + k, reps)}, device_id_type=MESH
        )

    loads = [
        pltpu.make_async_copy(src, dst, copy_sems.at[k])
        for k, (src, dst) in enumerate(
            (
                (lists_in.at[0, 0], lists),
                (list_counts_in.at[0], list_counts),
                (features_in, features),
                (adjacency_in.at[0, 0], adjacency),
                (tile_row_in, tile_row),
                (tile_column_in, tile_column),
                (tile_count_in, tile_count),
                (weight_in, weight),
                (cotangent_in, cotangent),
            )
        )
    ]
    for load in loads[:3]:
        load.start()
    loop(doms // 2, doms, greet_dom)
    loop(1, doms // 2, greet_dom)
    loop(1, reps, greet_rep)
    for load in loads[3:]:
        load.start()

    def push(src, dst, phase, target):
        pltpu.make_async_remote_copy(
            src_ref=src,
            dst_ref=dst,
            send_sem=send_sems.at[phase],
            recv_sem=recv_sems.at[phase],
            device_id=target,
            device_id_type=MESH,
        ).start()

    def await_bytes(ref, sems, phase):
        pltpu.make_async_copy(ref, ref, sems.at[phase]).wait()

    def send_block(block, src, dst, phase):
        def send(j):
            q = block * per + j

            @pl.when(q != d)
            def _():
                push(src.at[q], dst, phase, {"dom": q})

        loop(0, per, send)

    def far_block(b):
        step = (2 * lax.rem(b, 2) - 1) * ((b + 1) // 2)
        return lax.rem(d // per + blocks // 2 + step + 2 * blocks, blocks)

    far_reps = sorted(range(1, reps), key=lambda k: -min(k, reps - k))

    def share_rows(h, k, c):
        size = TILE // 2
        mine = row_grads[h].at[r, c * size : (c + 1) * size]
        push(mine, mine, GRAD + h, {"rep": lax.rem(r + k, reps)})

    lane = lax.broadcasted_iota(jnp.int32, (TILE, TILE), 1)
    row = lax.broadcasted_iota(jnp.int32, (TILE, TILE), 0)
    for load in loads[:3]:
        load.wait()
    slot = lax.broadcasted_iota(jnp.int32, (CAP, doms), 0)
    live_lists = jnp.where(slot < list_counts[...], lists[...], -1)
    for p in range(doms):
        listed[p // per, p % per * CAP : (p % per + 1) * CAP, :] = jnp.broadcast_to(
            live_lists[:, p : p + 1], (CAP, TILE)
        )

    def gather(block):
        rows_of = listed[block]
        onehot = jnp.concatenate(
            [jnp.where(rows_of == lane + i * TILE, 1.0, 0.0).astype(BF16) for i in range(row_tiles)],
            axis=1,
        )
        found = jnp.dot(onehot, features[...], preferred_element_type=F32).astype(BF16)
        for h in range(halves):
            outgoing[h, pl.ds(block * per, per)] = found[:, h * TILE : (h + 1) * TILE].reshape(
                per, CAP, TILE
            )

    def send_halo(block, h):
        send_block(block, outgoing.at[h], space[h].at[first_halo + d], HALO + h)

    loop(0, blocks, gather)
    pl.semaphore_wait(barrier, doms + reps - 2)
    for h in range(halves):
        loop(0, blocks, lambda b: send_halo(far_block(b), h))

    for load in loads[3:]:
        load.wait()
    for t in range(tiles):
        lanes = slice(t * TILE, (t + 1) * TILE)
        live = t < tile_count[0, 0]
        row_lanes[:, lanes] = jnp.full(
            (CAP, TILE), jnp.where(live, tile_row[0, 0, t], -1), jnp.int32
        )
        column_lanes[:, lanes] = jnp.full(
            (CAP, TILE), jnp.where(live, tile_column[0, 0, t], -1), jnp.int32
        )
        a_cat[:, :, lanes] = adjacency[t].reshape(per, CAP, TILE)
        at_cat[:, :, lanes] = adjacency[t].T.reshape(per, CAP, TILE)

    def mask_tiles(dst, values, lanes):
        def one(i):
            mask = jnp.where(lanes[...] == i, 1.0, 0.0).astype(BF16)
            dst[i] = (values[...] * mask[None]).reshape(TILE, tiles * TILE)

        loop(0, dst.shape[0], one)

    mask_tiles(by_row, a_cat, row_lanes)
    for h in range(halves):
        space[h][pl.ds(0, first_halo)] = features[:, h * TILE : (h + 1) * TILE].reshape(
            first_halo, CAP, TILE
        )
        space[h][first_halo + d] = jnp.zeros((CAP, TILE), BF16)
        back_recv[h, d] = jnp.zeros((CAP, TILE), BF16)
    mask_tiles(by_column, at_cat, column_lanes)

    def make_scatter(block):
        rows_of = listed[block].T
        for i in range(row_tiles):
            scatter[i, block] = jnp.where(rows_of == row + i * TILE, 1.0, 0.0).astype(BF16)

    loop(0, blocks, make_scatter)

    def tile_sum(values, h):
        return jnp.dot(values, picked[h], preferred_element_type=F32)

    pieces = 2
    piece_rows = TILE // pieces
    piece_at = [slice(c * piece_rows, (c + 1) * piece_rows) for c in range(pieces)]
    last = halves - 1

    def send_piece(h, i, c):
        push(
            agg_send.at[h, i, piece_at[c]],
            agg_recv.at[h, r, piece_at[c]],
            AGG_LAST + c if h == last else AGG + h,
            {"rep": i},
        )

    for h in range(halves):
        await_bytes(space[h].at[pl.ds(first_halo, doms - 1)], recv_sems, HALO + h)
        for t in range(tiles):
            picked[h, t * TILE : (t + 1) * TILE, :] = space[h][
                pl.ds(tile_column[0, 0, t] * per, per)
            ].reshape(TILE, TILE)
        for k in far_reps:
            i = lax.rem(r + k, reps)
            agg_send[h, i] = tile_sum(by_row[i], h).astype(BF16)
            if h == last:
                send_piece(h, i, 0)
            else:
                push(agg_send.at[h, i], agg_recv.at[h, r], AGG + h, {"rep": i})
        if h == last:
            for c in range(1, pieces):
                for k in far_reps:
                    send_piece(h, lax.rem(r + k, reps), c)
        own_sum[h] = tile_sum(by_row[r], h)

    for h in range(last):
        await_bytes(agg_recv.at[h, pl.ds(0, reps - 1)], recv_sems, AGG + h)
        for k in range(1, reps):
            own_sum[h] += agg_recv[h, lax.rem(r + k, reps)].astype(F32)
    for c in range(pieces):
        await_bytes(agg_recv.at[last, pl.ds(0, reps - 1), piece_at[c]], recv_sems, AGG_LAST + c)
        total = own_sum[last, piece_at[c]]
        for k in range(1, reps):
            total = total + agg_recv[last, lax.rem(r + k, reps), piece_at[c]].astype(F32)
        piece = jnp.concatenate(
            [own_sum[h, piece_at[c]].astype(BF16) for h in range(last)] + [total.astype(BF16)],
            axis=1,
        )
        aggregate[piece_at[c]] = piece
        pre_act = lax.dot_general(
            piece, weight[...], (((1,), (1,)), ((), ())), preferred_element_type=F32
        )
        activated, derivative = gelu_pair(pre_act)
        grad = (cotangent[piece_at[c]].astype(F32) * derivative).astype(BF16)
        pre_grad[piece_at[c]] = grad
        output[piece_at[c]] = activated.astype(BF16)
        row_grad = jnp.dot(grad, weight[...], preferred_element_type=F32).astype(BF16)
        for h in range(halves):
            row_grads[h][r, piece_at[c]] = row_grad[:, h * TILE : (h + 1) * TILE]
        for k in far_reps:
            share_rows(0, k, c)
    for h in range(1, halves):
        for c in range(pieces):
            for k in far_reps:
                share_rows(h, k, c)

    stores = [
        pltpu.make_async_copy(src, dst, copy_sems.at[len(loads) + k])
        for k, (src, dst) in enumerate(
            ((output, output_out), (weight_grad, weight_grad_out), (feature_grad, feature_grad_out))
        )
    ]
    stores[0].start()

    w_part = lax.dot_general(
        pre_grad[...], aggregate[...], (((0,), (0,)), ((), ())), preferred_element_type=F32
    )
    chunk = w_send.shape[1]
    half = doms // 2
    for h in range(2):
        w_send[h * half : (h + 1) * half] = w_part[:, h * TILE : (h + 1) * TILE].reshape(
            half, chunk, TILE
        )
    loop(0, blocks, lambda b: send_block(far_block(b), w_send, w_recv.at[d], W_DOM))
    w_recv[d] = w_send[d]

    def backward_local(h):
        def some(i):
            pair = by_column[pl.ds(2 * i, 2)].reshape(2 * TILE, tiles * TILE)
            feature_part[h, pl.ds(2 * i, 2)] = tile_sum(pair, h).reshape(2, TILE, TILE)

        loop(0, row_tiles // 2, some)

    group = 2 - blocks % 2
    for h in range(halves):
        await_bytes(row_grads[h].at[pl.ds(0, reps - 1)], recv_sems, GRAD + h)
        for t in range(tiles):
            picked[h, t * TILE : (t + 1) * TILE, :] = row_grads[h][tile_row[0, 0, t]]

        def backward_halo(b):
            some = [far_block(group * b + k) for k in range(group)]
            columns = jnp.concatenate([by_column[block + row_tiles] for block in some], axis=0)
            grads = tile_sum(columns, h).astype(BF16)
            for k, block in enumerate(some):
                back_send[h, pl.ds(block * per, per)] = grads[k * TILE : (k + 1) * TILE].reshape(
                    per, CAP, TILE
                )
                send_block(block, back_send.at[h], back_recv.at[h, d], BACK + h)

        loop(0, blocks // group, backward_halo)
        if h == 0:
            backward_local(h)

    spread = half // reps
    holder = lax.rem(d, half) // spread
    place = (d // half) * spread + lax.rem(d, spread)
    await_bytes(w_recv.at[pl.ds(0, doms - 1)], recv_sems, W_DOM)
    w_sum[...] = jnp.sum(w_recv[...], axis=0)

    @pl.when(r != holder)
    def _():
        push(w_sum, w_rep.at[r], W_REP, {"rep": holder})

    def finish_weight():
        @pl.when(r == holder)
        def _():
            await_bytes(w_rep.at[pl.ds(0, reps - 1)], recv_sems, W_REP)
            whole = w_sum[...]
            for k in range(1, reps):
                whole = whole + w_rep[lax.rem(r + k, reps)]
            w_done[place] = whole * scale

            def share_done(k):
                push(w_done.at[place], w_done.at[place], W_END, {"dom": lax.rem(d + k, doms)})

            loop(1, doms, share_done)

    own = []
    for h in range(halves):
        await_bytes(back_recv.at[h, pl.ds(0, doms - 1)], recv_sems, BACK + h)

        def feature_rows(i):
            total = feature_part[h, i]
            for block in range(blocks):
                returned = back_recv[h, block * per : (block + 1) * per].reshape(TILE, TILE)
                total = total + jnp.dot(scatter[i, block], returned, preferred_element_type=F32)
            return total

        for k in far_reps:
            i = lax.rem(r + k, reps)
            feat_send[h, i] = feature_rows(i).astype(BF16)
            push(feat_send.at[h, i], feat_recv.at[h, r], FEAT + h, {"rep": i})
        own.append(feature_rows(r))
        if h == 0:
            finish_weight()
        if h < last:
            backward_local(h + 1)

    @pl.when(r == holder)
    def _():
        await_bytes(w_done.at[pl.ds(0, 2 * spread - 1)], recv_sems, W_END)

    @pl.when(r != holder)
    def _():
        await_bytes(w_done, recv_sems, W_END)

    for h in range(2):
        weight_grad[:, h * TILE : (h + 1) * TILE] = w_done[h * spread : (h + 1) * spread].reshape(
            spread * chunk, TILE
        )
    stores[1].start()
    for h in range(halves):
        await_bytes(feat_recv.at[h, pl.ds(0, reps - 1)], recv_sems, FEAT + h)
        total = own[h]
        for k in range(1, reps):
            total = total + feat_recv[h, lax.rem(r + k, reps)].astype(F32)
        feature_grad[:, h * TILE : (h + 1) * TILE] = total.astype(BF16)

    stores[2].start()

    for h in range(halves):
        await_bytes(outgoing.at[h, pl.ds(0, doms - 1)], send_sems, HALO + h)
        if h != last:
            await_bytes(agg_send.at[h, pl.ds(0, reps - 1)], send_sems, AGG + h)
        await_bytes(row_grads[h].at[pl.ds(0, reps - 1)], send_sems, GRAD + h)
        await_bytes(back_send.at[h, pl.ds(0, doms - 1)], send_sems, BACK + h)
        await_bytes(feat_send.at[h, pl.ds(0, reps - 1)], send_sems, FEAT + h)
    for c in range(pieces):
        await_bytes(agg_send.at[last, pl.ds(0, reps - 1), piece_at[c]], send_sems, AGG_LAST + c)
    await_bytes(w_send.at[pl.ds(0, doms - 1)], send_sems, W_DOM)

    @pl.when(r != holder)
    def _():
        await_bytes(w_sum, send_sems, W_REP)

    @pl.when(r == holder)
    def _():
        await_bytes(w_send.at[pl.ds(0, doms - 1)], send_sems, W_END)

    for store in stores:
        store.wait()


def hand_over(*refs):
    made, results, held, sems = refs[:3], refs[3:6], refs[6:9], refs[9]
    loads = [pltpu.make_async_copy(made[k], held[k], sems.at[k]) for k in range(3)]
    stores = [pltpu.make_async_copy(held[k], results[k], sems.at[3 + k]) for k in range(3)]
    for load in loads:
        load.start()
    for load, store in zip(loads, stores):
        load.wait()
        store.start()
    for store in stores:
        store.wait()


def solution(mesh):
    doms, reps = mesh.shape["dom"], mesh.shape["rep"]

    def local(
        features,
        weight,
        adjacency,
        tile_row,
        tile_column,
        tile_counts,
        send_rows,
        send_counts,
        cotangent,
    ):
        rows, hidden = features.shape
        tiles = adjacency.shape[2]
        row_tiles = rows // TILE
        blocks = doms * CAP // TILE
        halves = hidden // TILE
        chunk = 2 * hidden // doms
        hbm = pl.BlockSpec(memory_space=pltpu.HBM)
        i32 = jnp.int32
        phases = halves * 5 + 5
        out_shape = (
            jax.ShapeDtypeStruct((rows // reps, hidden), BF16),
            jax.ShapeDtypeStruct((rows // reps, hidden), BF16),
            jax.ShapeDtypeStruct((hidden // reps, hidden), F32),
        )
        staged = [pltpu.VMEM(leaf.shape, leaf.dtype) for leaf in out_shape]
        scratch = (
            ((rows, hidden), BF16),
            ((hidden, hidden), BF16),
            ((tiles, TILE, TILE), BF16),
            ((CAP, doms), i32),
            ((1, doms), i32),
            (pltpu.SMEM, (1, 1, tiles), i32),
            (pltpu.SMEM, (1, 1, tiles), i32),
            (pltpu.SMEM, (1, 1), i32),
            ((rows // reps, hidden), BF16),
            ((blocks, TILE, TILE), i32),
            ((rows // CAP + doms, CAP, TILE), BF16),
            ((rows // CAP + doms, CAP, TILE), BF16),
            ((halves, doms, CAP, TILE), BF16),
            ((row_tiles, blocks, TILE, TILE), BF16),
            ((TILE // CAP, CAP, tiles * TILE), BF16),
            ((TILE // CAP, CAP, tiles * TILE), BF16),
            ((row_tiles, TILE, tiles * TILE), BF16),
            ((row_tiles + blocks, TILE, tiles * TILE), BF16),
            ((CAP, tiles * TILE), i32),
            ((CAP, tiles * TILE), i32),
            ((halves, tiles * TILE, TILE), BF16),
            ((halves, reps, TILE, TILE), BF16),
            ((halves, reps, TILE, TILE), BF16),
            ((halves, TILE, TILE), F32),
            ((TILE, hidden), BF16),
            ((TILE, hidden), BF16),
            ((reps, TILE, TILE), BF16),
            ((reps, TILE, TILE), BF16),
            ((halves, doms, CAP, TILE), BF16),
            ((halves, doms, CAP, TILE), BF16),
            ((halves, row_tiles, TILE, TILE), F32),
            ((halves, reps, TILE, TILE), BF16),
            ((halves, reps, TILE, TILE), BF16),
            ((doms, chunk, TILE), F32),
            ((doms, chunk, TILE), F32),
            ((chunk, TILE), F32),
            ((reps, chunk, TILE), F32),
            ((doms // reps, chunk, TILE), F32),
        )
        made = pl.pallas_call(
            functools.partial(kernel, doms, reps, float(rows * doms) ** (-0.5)),
            out_shape=out_shape,
            in_specs=[hbm] * 9,
            out_specs=(hbm,) * 3,
            scratch_shapes=staged
            + [
                item[0](*item[1:]) if len(item) == 3 else pltpu.VMEM(*item) for item in scratch
            ]
            + [
                pltpu.SemaphoreType.DMA((12,)),
                pltpu.SemaphoreType.DMA((phases,)),
                pltpu.SemaphoreType.DMA((phases,)),
            ],
            compiler_params=pltpu.CompilerParams(
                collective_id=0, has_side_effects=True, vmem_limit_bytes=60 * 2**20
            ),
        )(
            features,
            weight,
            adjacency,
            jnp.swapaxes(send_rows, 2, 3),
            send_counts,
            tile_row,
            tile_column,
            tile_counts,
            cotangent,
        )
        return pl.pallas_call(
            hand_over,
            out_shape=out_shape,
            in_specs=[hbm] * 3,
            out_specs=(hbm,) * 3,
            scratch_shapes=staged + [pltpu.SemaphoreType.DMA((6,))],
            compiler_params=pltpu.CompilerParams(vmem_limit_bytes=60 * 2**20),
        )(*made)

    in_specs = (
        P("dom", None),
        P(),
        P("dom", "rep", None, None, None),
        P("dom", "rep", None),
        P("dom", "rep", None),
        P("dom", "rep"),
        P("dom", "rep", None, None),
        P("dom", "rep", None),
        P(("dom", "rep"), None),
    )
    out_specs = (P(("dom", "rep"), None), P(("dom", "rep"), None), P("rep", None))
    return jax.shard_map(local, mesh=mesh, in_specs=in_specs, out_specs=out_specs, check_vma=False)
```

```python
import functools

import jax
import jax.numpy as jnp
from jax import lax
from jax.experimental import pallas as pl
from jax.experimental.pallas import tpu as pltpu
from jax.sharding import PartitionSpec as P

GELU_SCALE = 0.7978845608028654
GELU_CUBIC = 0.044715
MESH = pl.DeviceIdType.MESH
TILE = 128
CAP = 16
F32 = jnp.float32
BF16 = jnp.bfloat16


def gelu_pair(pre_act):
    inner_arg = GELU_SCALE * (pre_act + GELU_CUBIC * pre_act * pre_act * pre_act)
    tanh_part = jnp.tanh(inner_arg)
    activated = 0.5 * pre_act * (1.0 + tanh_part)
    derivative = 0.5 * (1.0 + tanh_part) + 0.5 * pre_act * (
        1.0 - tanh_part * tanh_part
    ) * GELU_SCALE * (1.0 + 3.0 * GELU_CUBIC * pre_act * pre_act)
    return (activated, derivative)


def loop(start, stop, body):
    def step(k, carry):
        body(k)
        return carry

    lax.fori_loop(start, stop, step, 0)


def kernel(
    doms,
    reps,
    scale,
    features_in,
    weight_in,
    adjacency_in,
    lists_in,
    list_counts_in,
    tile_row_in,
    tile_column_in,
    tile_count_in,
    cotangent_in,
    output_out,
    feature_grad_out,
    weight_grad_out,
    output,
    feature_grad,
    weight_grad,
    features,
    weight,
    adjacency,
    lists,
    list_counts,
    tile_row,
    tile_column,
    tile_count,
    cotangent,
    listed,
    space_low,
    space_high,
    outgoing,
    scatter,
    a_cat,
    at_cat,
    by_row,
    by_column,
    row_lanes,
    column_lanes,
    picked,
    agg_send,
    agg_recv,
    own_sum,
    aggregate,
    pre_grad,
    row_grads_low,
    row_grads_high,
    back_send,
    back_recv,
    feature_part,
    feat_send,
    feat_recv,
    w_send,
    w_recv,
    w_sum,
    w_rep,
    w_done,
    copy_sems,
    send_sems,
    recv_sems,
):
    d = lax.axis_index("dom")
    r = lax.axis_index("rep")
    rows, hidden = features.shape
    tiles = adjacency.shape[0]
    row_tiles = rows // TILE
    blocks = doms * CAP // TILE
    per = TILE // CAP
    first_halo = rows // CAP
    halves = hidden // TILE
    space = (space_low, space_high)
    row_grads = (row_grads_low, row_grads_high)
    HALO, AGG, GRAD, BACK, FEAT = (halves * k for k in range(5))
    W_DOM, W_REP, W_END, AGG_LAST = (halves * 5 + k for k in range(4))

    barrier = pltpu.get_barrier_semaphore()

    def greet_dom(k):
        pl.semaphore_signal(
            barrier, inc=1, device_id={"dom": lax.rem(d + k, doms)}, device_id_type=MESH
        )

    def greet_rep(k):
        pl.semaphore_signal(
            barrier, inc=1, device_id={"rep": lax.rem(r + k, reps)}, device_id_type=MESH
        )

    loads = [
        pltpu.make_async_copy(src, dst, copy_sems.at[k])
        for k, (src, dst) in enumerate(
            (
                (lists_in.at[0, 0], lists),
                (list_counts_in.at[0], list_counts),
                (features_in, features),
                (adjacency_in.at[0, 0], adjacency),
                (tile_row_in, tile_row),
                (tile_column_in, tile_column),
                (tile_count_in, tile_count),
                (weight_in, weight),
                (cotangent_in, cotangent),
            )
        )
    ]
    for load in loads[:3]:
        load.start()
    loop(doms // 2, doms, greet_dom)
    loop(1, doms // 2, greet_dom)
    loop(1, reps, greet_rep)
    for load in loads[3:]:
        load.start()

    def push(src, dst, phase, target):
        pltpu.make_async_remote_copy(
            src_ref=src,
            dst_ref=dst,
            send_sem=send_sems.at[phase],
            recv_sem=recv_sems.at[phase],
            device_id=target,
            device_id_type=MESH,
        ).start()

    def await_bytes(ref, sems, phase):
        pltpu.make_async_copy(ref, ref, sems.at[phase]).wait()

    def send_block(block, src, dst, phase):
        def send(j):
            q = block * per + j

            @pl.when(q != d)
            def _():
                push(src.at[q], dst, phase, {"dom": q})

        loop(0, per, send)

    def far_block(b):
        step = (2 * lax.rem(b, 2) - 1) * ((b + 1) // 2)
        return lax.rem(d // per + blocks // 2 + step + 2 * blocks, blocks)

    far_reps = sorted(range(1, reps), key=lambda k: -min(k, reps - k))

    def share_rows(h, k, c):
        size = TILE // 2
        mine = row_grads[h].at[r, c * size : (c + 1) * size]
        push(mine, mine, GRAD + h, {"rep": lax.rem(r + k, reps)})

    lane = lax.broadcasted_iota(jnp.int32, (TILE, TILE), 1)
    row = lax.broadcasted_iota(jnp.int32, (TILE, TILE), 0)
    for load in loads[:3]:
        load.wait()
    slot = lax.broadcasted_iota(jnp.int32, (CAP, doms), 0)
    live_lists = jnp.where(slot < list_counts[...], lists[...], -1)
    for p in range(doms):
        listed[p // per, p % per * CAP : (p % per + 1) * CAP, :] = jnp.broadcast_to(
            live_lists[:, p : p + 1], (CAP, TILE)
        )

    def gather(block):
        rows_of = listed[block]
        onehot = jnp.concatenate(
            [jnp.where(rows_of == lane + i * TILE, 1.0, 0.0).astype(BF16) for i in range(row_tiles)],
            axis=1,
        )
        found = jnp.dot(onehot, features[...], preferred_element_type=F32).astype(BF16)
        for h in range(halves):
            outgoing[h, pl.ds(block * per, per)] = found[:, h * TILE : (h + 1) * TILE].reshape(
                per, CAP, TILE
            )

    def send_halo(block, h):
        send_block(block, outgoing.at[h], space[h].at[first_halo + d], HALO + h)

    loop(0, blocks, gather)
    pl.semaphore_wait(barrier, doms + reps - 2)
    for h in range(halves):
        loop(0, blocks, lambda b: send_halo(far_block(b), h))

    for load in loads[3:]:
        load.wait()
    for t in range(tiles):
        lanes = slice(t * TILE, (t + 1) * TILE)
        live = t < tile_count[0, 0]
        row_lanes[:, lanes] = jnp.full(
            (CAP, TILE), jnp.where(live, tile_row[0, 0, t], -1), jnp.int32
        )
        column_lanes[:, lanes] = jnp.full(
            (CAP, TILE), jnp.where(live, tile_column[0, 0, t], -1), jnp.int32
        )
        a_cat[:, :, lanes] = adjacency[t].reshape(per, CAP, TILE)
        at_cat[:, :, lanes] = adjacency[t].T.reshape(per, CAP, TILE)

    def mask_tiles(dst, values, lanes):
        def one(i):
            mask = jnp.where(lanes[...] == i, 1.0, 0.0).astype(BF16)
            dst[i] = (values[...] * mask[None]).reshape(TILE, tiles * TILE)

        loop(0, dst.shape[0], one)

    mask_tiles(by_row, a_cat, row_lanes)
    for h in range(halves):
        space[h][pl.ds(0, first_halo)] = features[:, h * TILE : (h + 1) * TILE].reshape(
            first_halo, CAP, TILE
        )
        space[h][first_halo + d] = jnp.zeros((CAP, TILE), BF16)
        back_recv[h, d] = jnp.zeros((CAP, TILE), BF16)
    mask_tiles(by_column, at_cat, column_lanes)

    def make_scatter(block):
        rows_of = listed[block].T
        for i in range(row_tiles):
            scatter[i, :, pl.ds(pl.multiple_of(block * TILE, TILE), TILE)] = jnp.where(
                rows_of == row + i * TILE, 1.0, 0.0
            ).astype(BF16)

    loop(0, blocks, make_scatter)

    def tile_sum(values, h):
        return jnp.dot(values, picked[h], preferred_element_type=F32)

    pieces = 2
    piece_rows = TILE // pieces
    piece_at = [slice(c * piece_rows, (c + 1) * piece_rows) for c in range(pieces)]
    last = halves - 1

    def send_piece(h, i, c):
        push(
            agg_send.at[h, i, piece_at[c]],
            agg_recv.at[h, r, piece_at[c]],
            AGG_LAST + c if h == last else AGG + h,
            {"rep": i},
        )

    for h in range(halves):
        await_bytes(space[h].at[pl.ds(first_halo, doms - 1)], recv_sems, HALO + h)
        for t in range(tiles):
            picked[h, t * TILE : (t + 1) * TILE, :] = space[h][
                pl.ds(tile_column[0, 0, t] * per, per)
            ].reshape(TILE, TILE)
        for k in far_reps:
            i = lax.rem(r + k, reps)
            agg_send[h, i] = tile_sum(by_row[i], h).astype(BF16)
            if h == last:
                send_piece(h, i, 0)
            else:
                push(agg_send.at[h, i], agg_recv.at[h, r], AGG + h, {"rep": i})
        if h == last:
            for c in range(1, pieces):
                for k in far_reps:
                    send_piece(h, lax.rem(r + k, reps), c)
        own_sum[h] = tile_sum(by_row[r], h)

    for h in range(last):
        await_bytes(agg_recv.at[h, pl.ds(0, reps - 1)], recv_sems, AGG + h)
        for k in range(1, reps):
            own_sum[h] += agg_recv[h, lax.rem(r + k, reps)].astype(F32)
    for c in range(pieces):
        await_bytes(agg_recv.at[last, pl.ds(0, reps - 1), piece_at[c]], recv_sems, AGG_LAST + c)
        total = own_sum[last, piece_at[c]]
        for k in range(1, reps):
            total = total + agg_recv[last, lax.rem(r + k, reps), piece_at[c]].astype(F32)
        piece = jnp.concatenate(
            [own_sum[h, piece_at[c]].astype(BF16) for h in range(last)] + [total.astype(BF16)],
            axis=1,
        )
        aggregate[piece_at[c]] = piece
        pre_act = lax.dot_general(
            piece, weight[...], (((1,), (1,)), ((), ())), preferred_element_type=F32
        )
        activated, derivative = gelu_pair(pre_act)
        grad = (cotangent[piece_at[c]].astype(F32) * derivative).astype(BF16)
        pre_grad[piece_at[c]] = grad
        output[piece_at[c]] = activated.astype(BF16)
        row_grad = jnp.dot(grad, weight[...], preferred_element_type=F32).astype(BF16)
        for h in range(halves):
            row_grads[h][r, piece_at[c]] = row_grad[:, h * TILE : (h + 1) * TILE]
        for k in far_reps:
            share_rows(0, k, c)
    for h in range(1, halves):
        for c in range(pieces):
            for k in far_reps:
                share_rows(h, k, c)

    stores = [
        pltpu.make_async_copy(src, dst, copy_sems.at[len(loads) + k])
        for k, (src, dst) in enumerate(
            ((output, output_out), (weight_grad, weight_grad_out), (feature_grad, feature_grad_out))
        )
    ]
    stores[0].start()

    w_part = lax.dot_general(
        pre_grad[...], aggregate[...], (((0,), (0,)), ((), ())), preferred_element_type=F32
    )
    chunk = w_send.shape[1]
    half = doms // 2
    for h in range(2):
        w_send[h * half : (h + 1) * half] = w_part[:, h * TILE : (h + 1) * TILE].reshape(
            half, chunk, TILE
        )
    loop(0, blocks, lambda b: send_block(far_block(b), w_send, w_recv.at[d], W_DOM))
    w_recv[d] = w_send[d]

    def backward_local(h):
        def some(i):
            pair = by_column[pl.ds(2 * i, 2)].reshape(2 * TILE, tiles * TILE)
            feature_part[h, pl.ds(2 * i, 2)] = tile_sum(pair, h).reshape(2, TILE, TILE)

        loop(0, row_tiles // 2, some)

    group = 2 - blocks % 2
    for h in range(halves):
        await_bytes(row_grads[h].at[pl.ds(0, reps - 1)], recv_sems, GRAD + h)
        for t in range(tiles):
            picked[h, t * TILE : (t + 1) * TILE, :] = row_grads[h][tile_row[0, 0, t]]

        def backward_halo(b):
            some = [far_block(group * b + k) for k in range(group)]
            columns = jnp.concatenate([by_column[block + row_tiles] for block in some], axis=0)
            grads = tile_sum(columns, h).astype(BF16)
            for k, block in enumerate(some):
                back_send[h, pl.ds(block * per, per)] = grads[k * TILE : (k + 1) * TILE].reshape(
                    per, CAP, TILE
                )
                send_block(block, back_send.at[h], back_recv.at[h, d], BACK + h)

        loop(0, blocks // group, backward_halo)
        if h == 0:
            backward_local(h)

    spread = half // reps
    holder = lax.rem(d, half) // spread
    place = (d // half) * spread + lax.rem(d, spread)
    await_bytes(w_recv.at[pl.ds(0, doms - 1)], recv_sems, W_DOM)
    w_sum[...] = jnp.sum(w_recv[...], axis=0)

    @pl.when(r != holder)
    def _():
        push(w_sum, w_rep.at[r], W_REP, {"rep": holder})

    def finish_weight():
        @pl.when(r == holder)
        def _():
            await_bytes(w_rep.at[pl.ds(0, reps - 1)], recv_sems, W_REP)
            whole = w_sum[...]
            for k in range(1, reps):
                whole = whole + w_rep[lax.rem(r + k, reps)]
            w_done[place] = whole * scale

            def share_done(k):
                push(w_done.at[place], w_done.at[place], W_END, {"dom": lax.rem(d + k, doms)})

            loop(1, doms, share_done)

    own = []
    for h in range(halves):
        await_bytes(back_recv.at[h, pl.ds(0, doms - 1)], recv_sems, BACK + h)

        def feature_rows(i):
            returned = back_recv[h].reshape(doms * CAP, TILE)
            return feature_part[h, i] + jnp.dot(
                scatter[i], returned, preferred_element_type=F32
            )

        for k in far_reps:
            i = lax.rem(r + k, reps)
            feat_send[h, i] = feature_rows(i).astype(BF16)
            push(feat_send.at[h, i], feat_recv.at[h, r], FEAT + h, {"rep": i})
        own.append(feature_rows(r))
        if h == 0:
            finish_weight()
        if h < last:
            backward_local(h + 1)

    @pl.when(r == holder)
    def _():
        await_bytes(w_done.at[pl.ds(0, 2 * spread - 1)], recv_sems, W_END)

    @pl.when(r != holder)
    def _():
        await_bytes(w_done, recv_sems, W_END)

    for h in range(2):
        weight_grad[:, h * TILE : (h + 1) * TILE] = w_done[h * spread : (h + 1) * spread].reshape(
            spread * chunk, TILE
        )
    stores[1].start()
    for h in range(halves):
        await_bytes(feat_recv.at[h, pl.ds(0, reps - 1)], recv_sems, FEAT + h)
        total = own[h]
        for k in range(1, reps):
            total = total + feat_recv[h, lax.rem(r + k, reps)].astype(F32)
        feature_grad[:, h * TILE : (h + 1) * TILE] = total.astype(BF16)

    stores[2].start()

    for h in range(halves):
        await_bytes(outgoing.at[h, pl.ds(0, doms - 1)], send_sems, HALO + h)
        if h != last:
            await_bytes(agg_send.at[h, pl.ds(0, reps - 1)], send_sems, AGG + h)
        await_bytes(row_grads[h].at[pl.ds(0, reps - 1)], send_sems, GRAD + h)
        await_bytes(back_send.at[h, pl.ds(0, doms - 1)], send_sems, BACK + h)
        await_bytes(feat_send.at[h, pl.ds(0, reps - 1)], send_sems, FEAT + h)
    for c in range(pieces):
        await_bytes(agg_send.at[last, pl.ds(0, reps - 1), piece_at[c]], send_sems, AGG_LAST + c)
    await_bytes(w_send.at[pl.ds(0, doms - 1)], send_sems, W_DOM)

    @pl.when(r != holder)
    def _():
        await_bytes(w_sum, send_sems, W_REP)

    @pl.when(r == holder)
    def _():
        await_bytes(w_send.at[pl.ds(0, doms - 1)], send_sems, W_END)

    for store in stores:
        store.wait()


def hand_over(*refs):
    made, results, held, sems = refs[:3], refs[3:6], refs[6:9], refs[9]
    loads = [pltpu.make_async_copy(made[k], held[k], sems.at[k]) for k in range(3)]
    stores = [pltpu.make_async_copy(held[k], results[k], sems.at[3 + k]) for k in range(3)]
    for load in loads:
        load.start()
    for load, store in zip(loads, stores):
        load.wait()
        store.start()
    for store in stores:
        store.wait()


def solution(mesh):
    doms, reps = mesh.shape["dom"], mesh.shape["rep"]

    def local(
        features,
        weight,
        adjacency,
        tile_row,
        tile_column,
        tile_counts,
        send_rows,
        send_counts,
        cotangent,
    ):
        rows, hidden = features.shape
        tiles = adjacency.shape[2]
        row_tiles = rows // TILE
        blocks = doms * CAP // TILE
        halves = hidden // TILE
        chunk = 2 * hidden // doms
        hbm = pl.BlockSpec(memory_space=pltpu.HBM)
        i32 = jnp.int32
        phases = halves * 5 + 5
        out_shape = (
            jax.ShapeDtypeStruct((rows // reps, hidden), BF16),
            jax.ShapeDtypeStruct((rows // reps, hidden), BF16),
            jax.ShapeDtypeStruct((hidden // reps, hidden), F32),
        )
        staged = [pltpu.VMEM(leaf.shape, leaf.dtype) for leaf in out_shape]
        scratch = (
            ((rows, hidden), BF16),
            ((hidden, hidden), BF16),
            ((tiles, TILE, TILE), BF16),
            ((CAP, doms), i32),
            ((1, doms), i32),
            (pltpu.SMEM, (1, 1, tiles), i32),
            (pltpu.SMEM, (1, 1, tiles), i32),
            (pltpu.SMEM, (1, 1), i32),
            ((rows // reps, hidden), BF16),
            ((blocks, TILE, TILE), i32),
            ((rows // CAP + doms, CAP, TILE), BF16),
            ((rows // CAP + doms, CAP, TILE), BF16),
            ((halves, doms, CAP, TILE), BF16),
            ((row_tiles, TILE, doms * CAP), BF16),
            ((TILE // CAP, CAP, tiles * TILE), BF16),
            ((TILE // CAP, CAP, tiles * TILE), BF16),
            ((row_tiles, TILE, tiles * TILE), BF16),
            ((row_tiles + blocks, TILE, tiles * TILE), BF16),
            ((CAP, tiles * TILE), i32),
            ((CAP, tiles * TILE), i32),
            ((halves, tiles * TILE, TILE), BF16),
            ((halves, reps, TILE, TILE), BF16),
            ((halves, reps, TILE, TILE), BF16),
            ((halves, TILE, TILE), F32),
            ((TILE, hidden), BF16),
            ((TILE, hidden), BF16),
            ((reps, TILE, TILE), BF16),
            ((reps, TILE, TILE), BF16),
            ((halves, doms, CAP, TILE), BF16),
            ((halves, doms, CAP, TILE), BF16),
            ((halves, row_tiles, TILE, TILE), F32),
            ((halves, reps, TILE, TILE), BF16),
            ((halves, reps, TILE, TILE), BF16),
            ((doms, chunk, TILE), F32),
            ((doms, chunk, TILE), F32),
            ((chunk, TILE), F32),
            ((reps, chunk, TILE), F32),
            ((doms // reps, chunk, TILE), F32),
        )
        made = pl.pallas_call(
            functools.partial(kernel, doms, reps, float(rows * doms) ** (-0.5)),
            out_shape=out_shape,
            in_specs=[hbm] * 9,
            out_specs=(hbm,) * 3,
            scratch_shapes=staged
            + [
                item[0](*item[1:]) if len(item) == 3 else pltpu.VMEM(*item) for item in scratch
            ]
            + [
                pltpu.SemaphoreType.DMA((12,)),
                pltpu.SemaphoreType.DMA((phases,)),
                pltpu.SemaphoreType.DMA((phases,)),
            ],
            compiler_params=pltpu.CompilerParams(
                collective_id=0, has_side_effects=True, vmem_limit_bytes=60 * 2**20
            ),
        )(
            features,
            weight,
            adjacency,
            jnp.swapaxes(send_rows, 2, 3),
            send_counts,
            tile_row,
            tile_column,
            tile_counts,
            cotangent,
        )
        return pl.pallas_call(
            hand_over,
            out_shape=out_shape,
            in_specs=[hbm] * 3,
            out_specs=(hbm,) * 3,
            scratch_shapes=staged + [pltpu.SemaphoreType.DMA((6,))],
            compiler_params=pltpu.CompilerParams(vmem_limit_bytes=60 * 2**20),
        )(*made)

    in_specs = (
        P("dom", None),
        P(),
        P("dom", "rep", None, None, None),
        P("dom", "rep", None),
        P("dom", "rep", None),
        P("dom", "rep"),
        P("dom", "rep", None, None),
        P("dom", "rep", None),
        P(("dom", "rep"), None),
    )
    out_specs = (P(("dom", "rep"), None), P(("dom", "rep"), None), P("rep", None))
    return jax.shard_map(local, mesh=mesh, in_specs=in_specs, out_specs=out_specs, check_vma=False)
```

```python
import functools

import jax
import jax.numpy as jnp
from jax import lax
from jax.experimental import pallas as pl
from jax.experimental.pallas import tpu as pltpu
from jax.sharding import PartitionSpec as P

GELU_SCALE = 0.7978845608028654
GELU_CUBIC = 0.044715
MESH = pl.DeviceIdType.MESH
TILE = 128
CAP = 16
F32 = jnp.float32
BF16 = jnp.bfloat16


def gelu_pair(pre_act):
    inner_arg = GELU_SCALE * (pre_act + GELU_CUBIC * pre_act * pre_act * pre_act)
    tanh_part = jnp.tanh(inner_arg)
    activated = 0.5 * pre_act * (1.0 + tanh_part)
    derivative = 0.5 * (1.0 + tanh_part) + 0.5 * pre_act * (
        1.0 - tanh_part * tanh_part
    ) * GELU_SCALE * (1.0 + 3.0 * GELU_CUBIC * pre_act * pre_act)
    return (activated, derivative)


def loop(start, stop, body):
    def step(k, carry):
        body(k)
        return carry

    lax.fori_loop(start, stop, step, 0)


def kernel(
    doms,
    reps,
    scale,
    features_in,
    weight_in,
    adjacency_in,
    lists_in,
    list_counts_in,
    tile_row_in,
    tile_column_in,
    tile_count_in,
    cotangent_in,
    output_out,
    feature_grad_out,
    weight_grad_out,
    output,
    feature_grad,
    weight_grad,
    features,
    weight,
    adjacency,
    lists,
    list_counts,
    tile_row,
    tile_column,
    tile_count,
    cotangent,
    listed,
    space_low,
    space_high,
    outgoing,
    scatter,
    a_cat,
    at_cat,
    by_row,
    by_column,
    row_lanes,
    column_lanes,
    picked,
    agg_send,
    agg_recv,
    own_sum,
    aggregate,
    pre_grad,
    row_grads_low,
    row_grads_high,
    back_send,
    back_recv,
    feature_part,
    feat_send,
    feat_recv,
    w_send,
    w_recv,
    w_sum,
    w_rep,
    w_done,
    copy_sems,
    send_sems,
    recv_sems,
):
    d = lax.axis_index("dom")
    r = lax.axis_index("rep")
    rows, hidden = features.shape
    tiles = adjacency.shape[0]
    row_tiles = rows // TILE
    blocks = doms * CAP // TILE
    per = TILE // CAP
    first_halo = rows // CAP
    halves = hidden // TILE
    space = (space_low, space_high)
    row_grads = (row_grads_low, row_grads_high)
    HALO, AGG, GRAD, BACK, FEAT = (halves * k for k in range(5))
    W_DOM, W_REP, W_END, AGG_LAST = (halves * 5 + k for k in range(4))

    barrier = pltpu.get_barrier_semaphore()

    def greet_dom(k):
        pl.semaphore_signal(
            barrier, inc=1, device_id={"dom": lax.rem(d + k, doms)}, device_id_type=MESH
        )

    def greet_rep(k):
        pl.semaphore_signal(
            barrier, inc=1, device_id={"rep": lax.rem(r + k, reps)}, device_id_type=MESH
        )

    loads = [
        pltpu.make_async_copy(src, dst, copy_sems.at[k])
        for k, (src, dst) in enumerate(
            (
                (lists_in.at[0, 0], lists),
                (list_counts_in.at[0], list_counts),
                (features_in, features),
                (adjacency_in.at[0, 0], adjacency),
                (tile_row_in, tile_row),
                (tile_column_in, tile_column),
                (tile_count_in, tile_count),
                (weight_in, weight),
                (cotangent_in, cotangent),
            )
        )
    ]
    for load in loads[:3]:
        load.start()
    loop(doms // 2, doms, greet_dom)
    loop(1, doms // 2, greet_dom)
    loop(1, reps, greet_rep)
    for load in loads[3:]:
        load.start()

    def push(src, dst, phase, target):
        pltpu.make_async_remote_copy(
            src_ref=src,
            dst_ref=dst,
            send_sem=send_sems.at[phase],
            recv_sem=recv_sems.at[phase],
            device_id=target,
            device_id_type=MESH,
        ).start()

    def await_bytes(ref, sems, phase):
        pltpu.make_async_copy(ref, ref, sems.at[phase]).wait()

    def send_block(block, src, dst, phase):
        def send(j):
            q = block * per + j

            @pl.when(q != d)
            def _():
                push(src.at[q], dst, phase, {"dom": q})

        loop(0, per, send)

    def far_block(b):
        step = (2 * lax.rem(b, 2) - 1) * ((b + 1) // 2)
        return lax.rem(d // per + blocks // 2 + step + 2 * blocks, blocks)

    far_reps = sorted(range(1, reps), key=lambda k: -min(k, reps - k))

    def share_rows(h, k, c):
        size = TILE // 2
        mine = row_grads[h].at[r, c * size : (c + 1) * size]
        push(mine, mine, GRAD + h, {"rep": lax.rem(r + k, reps)})

    lane = lax.broadcasted_iota(jnp.int32, (TILE, TILE), 1)
    row = lax.broadcasted_iota(jnp.int32, (TILE, TILE), 0)
    for load in loads[:3]:
        load.wait()
    slot = lax.broadcasted_iota(jnp.int32, (CAP, doms), 0)
    live_lists = jnp.where(slot < list_counts[...], lists[...], -1)
    for p in range(doms):
        listed[p // per, p % per * CAP : (p % per + 1) * CAP, :] = jnp.broadcast_to(
            live_lists[:, p : p + 1], (CAP, TILE)
        )

    def gather(block):
        rows_of = listed[block]
        onehot = jnp.concatenate(
            [jnp.where(rows_of == lane + i * TILE, 1.0, 0.0).astype(BF16) for i in range(row_tiles)],
            axis=1,
        )
        found = jnp.dot(onehot, features[...], preferred_element_type=F32).astype(BF16)
        for h in range(halves):
            outgoing[h, pl.ds(block * per, per)] = found[:, h * TILE : (h + 1) * TILE].reshape(
                per, CAP, TILE
            )

    def send_halo(block, h):
        send_block(block, outgoing.at[h], space[h].at[first_halo + d], HALO + h)

    loop(0, blocks, gather)
    pl.semaphore_wait(barrier, doms + reps - 2)
    for h in range(halves):
        loop(0, blocks, lambda b: send_halo(far_block(b), h))

    for load in loads[3:]:
        load.wait()
    for t in range(tiles):
        lanes = slice(t * TILE, (t + 1) * TILE)
        live = t < tile_count[0, 0]
        row_lanes[:, lanes] = jnp.full(
            (CAP, TILE), jnp.where(live, tile_row[0, 0, t], -1), jnp.int32
        )
        column_lanes[:, lanes] = jnp.full(
            (CAP, TILE), jnp.where(live, tile_column[0, 0, t], -1), jnp.int32
        )
        a_cat[:, :, lanes] = adjacency[t].reshape(per, CAP, TILE)
        at_cat[:, :, lanes] = adjacency[t].T.reshape(per, CAP, TILE)

    def mask_tiles(dst, values, lanes):
        def one(i):
            mask = jnp.where(lanes[...] == i, 1.0, 0.0).astype(BF16)
            dst[i] = (values[...] * mask[None]).reshape(TILE, tiles * TILE)

        loop(0, dst.shape[0], one)

    mask_tiles(by_row, a_cat, row_lanes)
    for h in range(halves):
        space[h][pl.ds(0, first_halo)] = features[:, h * TILE : (h + 1) * TILE].reshape(
            first_halo, CAP, TILE
        )
        space[h][first_halo + d] = jnp.zeros((CAP, TILE), BF16)
        back_recv[h, d] = jnp.zeros((CAP, TILE), BF16)
    mask_tiles(by_column, at_cat, column_lanes)

    def make_scatter(block):
        rows_of = listed[block].T
        for i in range(row_tiles):
            scatter[i, :, pl.ds(pl.multiple_of(block * TILE, TILE), TILE)] = jnp.where(
                rows_of == row + i * TILE, 1.0, 0.0
            ).astype(BF16)

    loop(0, blocks, make_scatter)

    def tile_sum(values, h):
        return jnp.dot(values, picked[h], preferred_element_type=F32)

    pieces = 2
    piece_rows = TILE // pieces
    piece_at = [slice(c * piece_rows, (c + 1) * piece_rows) for c in range(pieces)]
    last = halves - 1

    def send_piece(h, i, c):
        push(
            agg_send.at[h, i, piece_at[c]],
            agg_recv.at[h, r, piece_at[c]],
            AGG_LAST + c if h == last else AGG + h,
            {"rep": i},
        )

    for h in range(halves):
        await_bytes(space[h].at[pl.ds(first_halo, doms - 1)], recv_sems, HALO + h)
        for t in range(tiles):
            picked[h, t * TILE : (t + 1) * TILE, :] = space[h][
                pl.ds(tile_column[0, 0, t] * per, per)
            ].reshape(TILE, TILE)
        for k in far_reps:
            i = lax.rem(r + k, reps)
            agg_send[h, i] = tile_sum(by_row[i], h).astype(BF16)
            if h == last:
                send_piece(h, i, 0)
            else:
                push(agg_send.at[h, i], agg_recv.at[h, r], AGG + h, {"rep": i})
        if h == last:
            for c in range(1, pieces):
                for k in far_reps:
                    send_piece(h, lax.rem(r + k, reps), c)
        own_sum[h] = tile_sum(by_row[r], h)

    for h in range(last):
        await_bytes(agg_recv.at[h, pl.ds(0, reps - 1)], recv_sems, AGG + h)
        for k in range(1, reps):
            own_sum[h] += agg_recv[h, lax.rem(r + k, reps)].astype(F32)
    for c in range(pieces):
        await_bytes(agg_recv.at[last, pl.ds(0, reps - 1), piece_at[c]], recv_sems, AGG_LAST + c)
        total = own_sum[last, piece_at[c]]
        for k in range(1, reps):
            total = total + agg_recv[last, lax.rem(r + k, reps), piece_at[c]].astype(F32)
        piece = jnp.concatenate(
            [own_sum[h, piece_at[c]].astype(BF16) for h in range(last)] + [total.astype(BF16)],
            axis=1,
        )
        aggregate[piece_at[c]] = piece
        pre_act = lax.dot_general(
            piece, weight[...], (((1,), (1,)), ((), ())), preferred_element_type=F32
        )
        activated, derivative = gelu_pair(pre_act)
        grad = (cotangent[piece_at[c]].astype(F32) * derivative).astype(BF16)
        pre_grad[piece_at[c]] = grad
        output[piece_at[c]] = activated.astype(BF16)
        row_grad = jnp.dot(grad, weight[...], preferred_element_type=F32).astype(BF16)
        for h in range(halves):
            row_grads[h][r, piece_at[c]] = row_grad[:, h * TILE : (h + 1) * TILE]
        for k in far_reps:
            share_rows(0, k, c)
    for h in range(1, halves):
        for k in far_reps:
            mine = row_grads[h].at[r]
            push(mine, mine, GRAD + h, {"rep": lax.rem(r + k, reps)})

    stores = [
        pltpu.make_async_copy(src, dst, copy_sems.at[len(loads) + k])
        for k, (src, dst) in enumerate(
            ((output, output_out), (weight_grad, weight_grad_out), (feature_grad, feature_grad_out))
        )
    ]
    stores[0].start()

    w_part = lax.dot_general(
        pre_grad[...], aggregate[...], (((0,), (0,)), ((), ())), preferred_element_type=F32
    )
    chunk = w_send.shape[1]
    half = doms // 2
    for h in range(2):
        w_send[h * half : (h + 1) * half] = w_part[:, h * TILE : (h + 1) * TILE].reshape(
            half, chunk, TILE
        )
    loop(0, blocks, lambda b: send_block(far_block(b), w_send, w_recv.at[d], W_DOM))
    w_recv[d] = w_send[d]

    def backward_local(h):
        def some(i):
            pair = by_column[pl.ds(2 * i, 2)].reshape(2 * TILE, tiles * TILE)
            feature_part[h, pl.ds(2 * i, 2)] = tile_sum(pair, h).reshape(2, TILE, TILE)

        loop(0, row_tiles // 2, some)

    group = 2 - blocks % 2
    for h in range(halves):
        await_bytes(row_grads[h].at[pl.ds(0, reps - 1)], recv_sems, GRAD + h)
        for t in range(tiles):
            picked[h, t * TILE : (t + 1) * TILE, :] = row_grads[h][tile_row[0, 0, t]]

        def backward_halo(b):
            some = [far_block(group * b + k) for k in range(group)]
            columns = jnp.concatenate([by_column[block + row_tiles] for block in some], axis=0)
            grads = tile_sum(columns, h).astype(BF16)
            for k, block in enumerate(some):
                back_send[h, pl.ds(block * per, per)] = grads[k * TILE : (k + 1) * TILE].reshape(
                    per, CAP, TILE
                )
                send_block(block, back_send.at[h], back_recv.at[h, d], BACK + h)

        loop(0, blocks // group, backward_halo)
        if h == 0:
            backward_local(h)

    spread = half // reps
    holder = lax.rem(d, half) // spread
    place = (d // half) * spread + lax.rem(d, spread)
    await_bytes(w_recv.at[pl.ds(0, doms - 1)], recv_sems, W_DOM)
    w_sum[...] = jnp.sum(w_recv[...], axis=0)

    @pl.when(r != holder)
    def _():
        push(w_sum, w_rep.at[r], W_REP, {"rep": holder})

    def finish_weight():
        @pl.when(r == holder)
        def _():
            await_bytes(w_rep.at[pl.ds(0, reps - 1)], recv_sems, W_REP)
            whole = w_sum[...]
            for k in range(1, reps):
                whole = whole + w_rep[lax.rem(r + k, reps)]
            w_done[place] = whole * scale

            def share_done(k):
                push(w_done.at[place], w_done.at[place], W_END, {"dom": lax.rem(d + k, doms)})

            loop(1, doms, share_done)

    own = []
    for h in range(halves):
        await_bytes(back_recv.at[h, pl.ds(0, doms - 1)], recv_sems, BACK + h)

        def feature_rows(i):
            returned = back_recv[h].reshape(doms * CAP, TILE)
            return feature_part[h, i] + jnp.dot(
                scatter[i], returned, preferred_element_type=F32
            )

        for k in far_reps:
            i = lax.rem(r + k, reps)
            feat_send[h, i] = feature_rows(i).astype(BF16)
            push(feat_send.at[h, i], feat_recv.at[h, r], FEAT + h, {"rep": i})
        own.append(feature_rows(r))
        if h == 0:
            finish_weight()
        if h < last:
            backward_local(h + 1)

    @pl.when(r == holder)
    def _():
        await_bytes(w_done.at[pl.ds(0, 2 * spread - 1)], recv_sems, W_END)

    @pl.when(r != holder)
    def _():
        await_bytes(w_done, recv_sems, W_END)

    for h in range(2):
        weight_grad[:, h * TILE : (h + 1) * TILE] = w_done[h * spread : (h + 1) * spread].reshape(
            spread * chunk, TILE
        )
    stores[1].start()
    for h in range(halves):
        await_bytes(feat_recv.at[h, pl.ds(0, reps - 1)], recv_sems, FEAT + h)
        total = own[h]
        for k in range(1, reps):
            total = total + feat_recv[h, lax.rem(r + k, reps)].astype(F32)
        feature_grad[:, h * TILE : (h + 1) * TILE] = total.astype(BF16)

    stores[2].start()

    for h in range(halves):
        await_bytes(outgoing.at[h, pl.ds(0, doms - 1)], send_sems, HALO + h)
        if h != last:
            await_bytes(agg_send.at[h, pl.ds(0, reps - 1)], send_sems, AGG + h)
        await_bytes(row_grads[h].at[pl.ds(0, reps - 1)], send_sems, GRAD + h)
        await_bytes(back_send.at[h, pl.ds(0, doms - 1)], send_sems, BACK + h)
        await_bytes(feat_send.at[h, pl.ds(0, reps - 1)], send_sems, FEAT + h)
    for c in range(pieces):
        await_bytes(agg_send.at[last, pl.ds(0, reps - 1), piece_at[c]], send_sems, AGG_LAST + c)
    await_bytes(w_send.at[pl.ds(0, doms - 1)], send_sems, W_DOM)

    @pl.when(r != holder)
    def _():
        await_bytes(w_sum, send_sems, W_REP)

    @pl.when(r == holder)
    def _():
        await_bytes(w_send.at[pl.ds(0, doms - 1)], send_sems, W_END)

    for store in stores:
        store.wait()


def hand_over(*refs):
    made, results, held, sems = refs[:3], refs[3:6], refs[6:9], refs[9]
    loads = [pltpu.make_async_copy(made[k], held[k], sems.at[k]) for k in range(3)]
    stores = [pltpu.make_async_copy(held[k], results[k], sems.at[3 + k]) for k in range(3)]
    for load in loads:
        load.start()
    for load, store in zip(loads, stores):
        load.wait()
        store.start()
    for store in stores:
        store.wait()


def solution(mesh):
    doms, reps = mesh.shape["dom"], mesh.shape["rep"]

    def local(
        features,
        weight,
        adjacency,
        tile_row,
        tile_column,
        tile_counts,
        send_rows,
        send_counts,
        cotangent,
    ):
        rows, hidden = features.shape
        tiles = adjacency.shape[2]
        row_tiles = rows // TILE
        blocks = doms * CAP // TILE
        halves = hidden // TILE
        chunk = 2 * hidden // doms
        hbm = pl.BlockSpec(memory_space=pltpu.HBM)
        i32 = jnp.int32
        phases = halves * 5 + 5
        out_shape = (
            jax.ShapeDtypeStruct((rows // reps, hidden), BF16),
            jax.ShapeDtypeStruct((rows // reps, hidden), BF16),
            jax.ShapeDtypeStruct((hidden // reps, hidden), F32),
        )
        staged = [pltpu.VMEM(leaf.shape, leaf.dtype) for leaf in out_shape]
        scratch = (
            ((rows, hidden), BF16),
            ((hidden, hidden), BF16),
            ((tiles, TILE, TILE), BF16),
            ((CAP, doms), i32),
            ((1, doms), i32),
            (pltpu.SMEM, (1, 1, tiles), i32),
            (pltpu.SMEM, (1, 1, tiles), i32),
            (pltpu.SMEM, (1, 1), i32),
            ((rows // reps, hidden), BF16),
            ((blocks, TILE, TILE), i32),
            ((rows // CAP + doms, CAP, TILE), BF16),
            ((rows // CAP + doms, CAP, TILE), BF16),
            ((halves, doms, CAP, TILE), BF16),
            ((row_tiles, TILE, doms * CAP), BF16),
            ((TILE // CAP, CAP, tiles * TILE), BF16),
            ((TILE // CAP, CAP, tiles * TILE), BF16),
            ((row_tiles, TILE, tiles * TILE), BF16),
            ((row_tiles + blocks, TILE, tiles * TILE), BF16),
            ((CAP, tiles * TILE), i32),
            ((CAP, tiles * TILE), i32),
            ((halves, tiles * TILE, TILE), BF16),
            ((halves, reps, TILE, TILE), BF16),
            ((halves, reps, TILE, TILE), BF16),
            ((halves, TILE, TILE), F32),
            ((TILE, hidden), BF16),
            ((TILE, hidden), BF16),
            ((reps, TILE, TILE), BF16),
            ((reps, TILE, TILE), BF16),
            ((halves, doms, CAP, TILE), BF16),
            ((halves, doms, CAP, TILE), BF16),
            ((halves, row_tiles, TILE, TILE), F32),
            ((halves, reps, TILE, TILE), BF16),
            ((halves, reps, TILE, TILE), BF16),
            ((doms, chunk, TILE), F32),
            ((doms, chunk, TILE), F32),
            ((chunk, TILE), F32),
            ((reps, chunk, TILE), F32),
            ((doms // reps, chunk, TILE), F32),
        )
        made = pl.pallas_call(
            functools.partial(kernel, doms, reps, float(rows * doms) ** (-0.5)),
            out_shape=out_shape,
            in_specs=[hbm] * 9,
            out_specs=(hbm,) * 3,
            scratch_shapes=staged
            + [
                item[0](*item[1:]) if len(item) == 3 else pltpu.VMEM(*item) for item in scratch
            ]
            + [
                pltpu.SemaphoreType.DMA((12,)),
                pltpu.SemaphoreType.DMA((phases,)),
                pltpu.SemaphoreType.DMA((phases,)),
            ],
            compiler_params=pltpu.CompilerParams(
                collective_id=0, has_side_effects=True, vmem_limit_bytes=60 * 2**20
            ),
        )(
            features,
            weight,
            adjacency,
            jnp.swapaxes(send_rows, 2, 3),
            send_counts,
            tile_row,
            tile_column,
            tile_counts,
            cotangent,
        )
        return pl.pallas_call(
            hand_over,
            out_shape=out_shape,
            in_specs=[hbm] * 3,
            out_specs=(hbm,) * 3,
            scratch_shapes=staged + [pltpu.SemaphoreType.DMA((6,))],
            compiler_params=pltpu.CompilerParams(vmem_limit_bytes=60 * 2**20),
        )(*made)

    in_specs = (
        P("dom", None),
        P(),
        P("dom", "rep", None, None, None),
        P("dom", "rep", None),
        P("dom", "rep", None),
        P("dom", "rep"),
        P("dom", "rep", None, None),
        P("dom", "rep", None),
        P(("dom", "rep"), None),
    )
    out_specs = (P(("dom", "rep"), None), P(("dom", "rep"), None), P("rep", None))
    return jax.shard_map(local, mesh=mesh, in_specs=in_specs, out_specs=out_specs, check_vma=False)
```
